32 devices in a mesh: ctx: 16 (over z, x, core), tp: 2 (over y).
Axes of the slice: x: 2, y: 2, z: 4, core: 2. Of those that a mesh axis runs over, the one named last changes fastest.
Arguments:
- tokens: bfloat16 [2048, 2048], P('ctx'), may hold values from -6 to 6
- block_ids: int32 [32], replicated, may hold values from 0 to 31, as said below
- gain_attn: bfloat16 [2048], P('ctx'), may hold values from 0.099609375 to 1.8984375
- w_query: bfloat16 [2048, 2048], P('ctx', 'tp'), may hold values from -0.25 to 0.25
- key_weight: bfloat16 [2048, 512], P('ctx', 'tp'), may hold values from -0.125 to 0.125
- value_weight: bfloat16 [2048, 512], P('ctx', 'tp'), may hold values from -0.125 to 0.125
- w_out: bfloat16 [2048, 2048], P('ctx', 'tp'), may hold values from -1 to 1
- gain_mlp: bfloat16 [2048], P('ctx'), may hold values from 0.099609375 to 1.8984375
- w_gate: bfloat16 [2048, 8192], P('ctx', 'tp'), may hold values from -0.125 to 0.125
- w_up: bfloat16 [2048, 8192], P('ctx', 'tp'), may hold values from -0.125 to 0.125
- w_down: bfloat16 [2048, 8192], P('ctx', 'tp'), may hold values from -0.0625 to 0.0625
- cotangent: bfloat16 [2048, 2048], P('ctx'), may hold values from -6 to 6
Outputs:
- block_out: bfloat16 [2048, 2048], P('ctx')
- input_gradient: bfloat16 [2048, 2048], P('ctx')
- gain_attn_gradient: float32 [2048], P('ctx')
- query_gradient: float32 [2048, 2048], P('ctx', 'tp')
- key_gradient: float32 [2048, 512], P('ctx', 'tp')
- value_gradient: float32 [2048, 512], P('ctx', 'tp')
- out_gradient: float32 [2048, 2048], P('ctx', 'tp')
- gain_mlp_gradient: float32 [2048], P('ctx')
- gate_gradient: float32 [2048, 8192], P('ctx', 'tp')
- up_gradient: float32 [2048, 8192], P('ctx', 'tp')
- down_gradient: float32 [2048, 8192], P('ctx', 'tp')
The draws below stay inside these ranges and needn't reach their ends.
Inputs may be any that keep to these rules, and one draw needn't show every extreme that they name: `block_ids`: each block number 0 to 31 stands once; the two places of one index of ctx hold block numbers that add up to 31.
All inputs are finite; a program needn't handle non-finite values.
Results may differ from the reference program's by a relative error of at most 0.019.
The reference program's roundings to bfloat16 on the way count: a program that leaves them out, or rounds other values in their place, can miss the bound.
Values may be sent and summed in bfloat16 or wider, within the bound.
A program may use at most 576 MiB of HBM per device.

```python
import math
import jax
import jax.numpy as jnp
from jax import lax

MODEL_DIM = 2048
QUERY_HEADS = 32
KEY_VALUE_HEADS = 8
HEAD_DIM = 64
FF = 8192
BLOCK = 64
TOK_DEV = 128
SEQ = 2048


def draw_block_ids(key, part):
    key = jax.random.fold_in(key, 11)
    pairs = SEQ // TOK_DEV
    order = jax.random.permutation(jax.random.fold_in(key, 1), pairs).astype(jnp.int32)
    flips = jax.random.randint(jax.random.fold_in(key, 2), (pairs,), 0, 2).astype(jnp.int32)
    first = jnp.where(flips == 1, 2 * pairs - 1 - order, order).astype(jnp.int32)
    second = (2 * pairs - 1 - first).astype(jnp.int32)
    return jnp.stack([first, second], axis=1).reshape(2 * pairs)


def block_scale(own_key, extent, pieces, least, largest):
    def one(position, shards_of):
        draws = jax.random.uniform(jax.random.fold_in(jax.random.fold_in(own_key, 6), position), (shards_of,), jnp.float32, least / len(pieces), largest / len(pieces))
        return jnp.repeat(jnp.exp(draws), extent[position] // shards_of).reshape((-1,) + (1,) * (len(extent) - position - 1))

    loudness = one(*pieces[0])
    for cut in pieces[1:]:
        loudness = loudness * one(*cut)
    return loudness


def noise(stream_key, shape, spread, bound, cuts=(), kind=jnp.bfloat16):
    drawn = spread * jax.random.normal(stream_key, shape, jnp.float32)
    if cuts:
        drawn = drawn * block_scale(stream_key, shape, cuts, -0.22, 0.18)
    return jnp.clip(drawn, -bound, bound).astype(kind)


def setup_inputs(seed: int = 0) -> dict:
    key_list = jax.random.split(jax.random.key(seed), 13)
    return {
        "tokens": noise(key_list[0], (SEQ, MODEL_DIM), 1.0, 6.0, ((0, 16),)),
        "block_ids": draw_block_ids(jax.random.fold_in(key_list[12], 71), 0),
        "gain_attn": jnp.clip(1.0 + 0.18 * jax.random.normal(key_list[2], (MODEL_DIM,), jnp.float32), 0.099609375, 1.8984375).astype(jnp.bfloat16),
        "w_query": noise(key_list[3], (MODEL_DIM, QUERY_HEADS * HEAD_DIM), (MODEL_DIM // 4) ** -0.5, 0.25, ((0, 16), (1, 2))),
        "key_weight": noise(key_list[4], (MODEL_DIM, KEY_VALUE_HEADS * HEAD_DIM), MODEL_DIM ** -0.5, 0.125, ((0, 16), (1, 2))),
        "value_weight": noise(key_list[5], (MODEL_DIM, KEY_VALUE_HEADS * HEAD_DIM), MODEL_DIM ** -0.5, 0.125, ((0, 16), (1, 2))),
        "w_out": noise(key_list[6], (MODEL_DIM, QUERY_HEADS * HEAD_DIM), (QUERY_HEADS * HEAD_DIM // 64) ** -0.5, 1.0, ((0, 16), (1, 2))),
        "gain_mlp": jnp.clip(1.0 + 0.18 * jax.random.normal(key_list[7], (MODEL_DIM,), jnp.float32), 0.099609375, 1.8984375).astype(jnp.bfloat16),
        "w_gate": noise(key_list[8], (MODEL_DIM, FF), MODEL_DIM ** -0.5, 0.125, ((0, 16), (1, 2))),
        "w_up": noise(key_list[9], (MODEL_DIM, FF), MODEL_DIM ** -0.5, 0.125, ((0, 16), (1, 2))),
        "w_down": noise(key_list[10], (MODEL_DIM, FF), FF ** -0.5, 0.0625, ((0, 16), (1, 2))),
        "cotangent": noise(key_list[11], (SEQ, MODEL_DIM), 1.0, 6.0, ((0, 16),)),
    }


EPS = 1e-05
THETA = 500000.0
NEG = -1e+30
HIGH = lax.Precision.HIGHEST

@jax.custom_vjp
def reduced_precision(v):
    return lax.optimization_barrier(v.astype(jnp.bfloat16)).astype(jnp.float32)

@jax.custom_vjp
def reduced_backward(v):
    return v

def low_keep(v):
    return (reduced_precision(v), None)

def low_pass(kept, grad):
    return (grad,)

def back_keep(v):
    return (v, None)

def back_low(kept, grad):
    return (reduced_precision(grad),)
reduced_precision.defvjp(low_keep, low_pass)
reduced_backward.defvjp(back_keep, back_low)

def turned(tensor):
    half_width = tensor.shape[-1] // 2
    return jnp.concatenate([-tensor[..., half_width:], tensor[..., :half_width]], axis=-1)

def rotary_embed(tensor, cosine_table, sine_table):
    return tensor * cosine_table[:, None, :] + turned(tensor) * sine_table[:, None, :]

def rope_tables(token_positions, head_width):
    half_width = head_width // 2
    frequencies = THETA ** (-(jnp.arange(half_width, dtype=jnp.float32) * 2.0 / head_width))
    angles = token_positions.astype(jnp.float32)[:, None] * frequencies[None, :]
    angles = jnp.concatenate([angles, angles], axis=1)
    return (jnp.cos(angles), jnp.sin(angles))

def rms_scale(values, gain_vec):
    return values * lax.rsqrt(lax.optimization_barrier(jnp.mean(values * values, axis=-1, keepdims=True)) + EPS) * gain_vec

def attention_layer(query_rotated, key_rotated, value_all, token_positions):
    sequence_length = query_rotated.shape[0]
    row_block_size = math.gcd(sequence_length, 512)
    group_length = QUERY_HEADS // KEY_VALUE_HEADS
    query_block_list = query_rotated.reshape(sequence_length // row_block_size, row_block_size, KEY_VALUE_HEADS, group_length, HEAD_DIM)
    pos_blocks = token_positions.reshape(sequence_length // row_block_size, row_block_size)

    def one_block(element):
        q_part, pos_part = element
        scores = reduced_backward(jnp.einsum('qkgd,skd->kgqs', q_part, key_rotated, precision=HIGH) * HEAD_DIM ** (-0.5))
        allowed = token_positions[None, :] <= pos_part[:, None]
        scores = jnp.where(allowed[None, None], scores, NEG)
        row_max = lax.optimization_barrier(jnp.max(scores, axis=-1, keepdims=True))
        exponent = jnp.exp(scores - row_max)
        softmaxed = reduced_precision(exponent / lax.optimization_barrier(jnp.sum(exponent, axis=-1, keepdims=True)))
        return jnp.einsum('kgqs,skd->qkgd', softmaxed, value_all, precision=HIGH)
    mixed_heads = lax.map(jax.checkpoint(one_block), (query_block_list, pos_blocks))
    return mixed_heads.reshape(sequence_length, QUERY_HEADS * HEAD_DIM)

def forward(inputs, gain_attn, w_query, key_weight, value_weight, w_out, gain_mlp, w_gate, w_up, w_down, token_positions):
    sequence_length = inputs.shape[0]
    cosine_table, sine_table = rope_tables(token_positions, HEAD_DIM)
    normed_attn = reduced_precision(rms_scale(inputs, gain_attn))
    query_lin = reduced_backward(jnp.dot(normed_attn, w_query, precision=HIGH))
    key_linear = reduced_backward(jnp.dot(normed_attn, key_weight, precision=HIGH))
    value_linear = reduced_precision(reduced_backward(jnp.dot(normed_attn, value_weight, precision=HIGH)))
    query_rotated = reduced_precision(rotary_embed(query_lin.reshape(sequence_length, QUERY_HEADS, HEAD_DIM), cosine_table, sine_table))
    key_rotated = reduced_precision(rotary_embed(key_linear.reshape(sequence_length, KEY_VALUE_HEADS, HEAD_DIM), cosine_table, sine_table))
    mixed_heads = reduced_backward(reduced_precision(attention_layer(query_rotated, key_rotated, value_linear.reshape(sequence_length, KEY_VALUE_HEADS, HEAD_DIM), token_positions)))
    attn_out = reduced_backward(jnp.dot(mixed_heads, w_out.T, precision=HIGH))
    residual = inputs + attn_out
    normed_mlp = reduced_precision(rms_scale(residual, gain_mlp))
    gate_pre = reduced_backward(jnp.dot(normed_mlp, w_gate, precision=HIGH))
    up_pre = reduced_backward(jnp.dot(normed_mlp, w_up, precision=HIGH))
    hidden = reduced_precision(jax.nn.silu(gate_pre) * up_pre)
    return residual + jnp.dot(hidden, w_down.T, precision=HIGH)

def reference(tokens, block_ids, gain_attn, w_query, key_weight, value_weight, w_out, gain_mlp, w_gate, w_up, w_down, cotangent):
    offsets = jnp.arange(BLOCK, dtype=jnp.int32)
    token_positions = (block_ids.astype(jnp.int32)[:, None] * BLOCK + offsets[None, :]).reshape(SEQ).astype(jnp.int32)
    arrays = (tokens, gain_attn, w_query, key_weight, value_weight, w_out, gain_mlp, w_gate, w_up, w_down)
    arrays = tuple((element.astype(jnp.float32) for element in arrays))

    def wrapped(*inner):
        return forward(*inner, token_positions)
    result, pullback = jax.vjp(wrapped, *arrays)
    grads = pullback(cotangent.astype(jnp.float32))
    return (result.astype(jnp.bfloat16), grads[0].astype(jnp.bfloat16), grads[1], grads[2], grads[3], grads[4], grads[5], grads[6], grads[7], grads[8], grads[9])
```

```python
import math

import jax
import jax.numpy as jnp
from jax import lax
from jax.experimental import pallas as pl
from jax.experimental.pallas import tpu as pltpu
from jax.sharding import Mesh
from jax.sharding import PartitionSpec as P

HEAD_DIM = 64
BLOCK = 64
EPS = 1e-05
THETA = 500000.0
NEG = -1e30
MESH = pl.DeviceIdType.MESH
AXES = ("yh", "z", "x", "core", "tp")
NN = (((1,), (0,)), ((), ()))
NT = (((1,), (1,)), ((), ()))
TN = (((0,), (0,)), ((), ()))
F32 = jnp.float32
BF16 = jnp.bfloat16
CHUNKS = 4
TMP = 256


def dot(a, b, dims):
    return lax.dot_general(a, b, dims, preferred_element_type=F32)


def mod(a, n):
    return lax.rem(a, jnp.int32(n))


class Sems:
    def __init__(self):
        self.size = 0

    def take(self, count):
        first = self.size
        self.size += count
        return first


class Plan:
    def __init__(self, sizes, model, heads_cols, kv_cols, hidden_cols, tokens):
        self.YH, self.Z, self.X, self.TP = sizes
        self.n_ctx = self.YH * self.Z * self.X * 2
        self.n_dev = self.n_ctx * self.TP
        self.S = self.YH * self.X * 2
        self.R = model // self.n_ctx
        self.model = model
        self.qc = heads_cols // self.Z
        self.kc = kv_cols // self.Z
        self.fc = hidden_cols // self.Z
        self.cols = [self.qc + 2 * self.kc, self.qc, self.fc, self.fc, self.fc]
        self.half = tokens // 2
        self.rows = 2 * self.Z * self.half
        self.seq = self.S * self.rows
        self.nseg = self.n_ctx // 2
        self.tile = 256 if self.seq <= 2048 else 128
        send, recv, local = Sems(), Sems(), Sems()
        W, Z, S, YX = 5, self.Z, self.S, self.YH * self.X
        self.gain_s, self.gain_r = send.take(self.n_ctx), recv.take(1)
        self.swap_s, self.swap_r = send.take(2), recv.take(2)
        self.s1_s, self.s1_r, self.s1_l = send.take(W * Z), recv.take(W * Z * 2), local.take(W)
        self.s2_s, self.s2_r = send.take(W * Z * S), recv.take(W * YX * Z)
        self.ag_s, self.ag_r = send.take(4 * 2 * Z), recv.take(4 * 2 * Z)
        self.rb_s, self.rb_r = send.take(4 * CHUNKS), recv.take(4 * CHUNKS)
        self.rz_s, self.rz_r = send.take(4 * CHUNKS * Z), recv.take(4 * CHUNKS * Z)
        self.kv_s, self.kv_r = send.take(S), recv.take(S)
        self.dkv_s, self.dkv_r = send.take(S), recv.take(S)
        self.dw_s, self.dw_r = send.take(W * self.nseg), recv.take(W * S * Z)
        self.og_s, self.og_r = send.take(W * Z * 2), recv.take(W * Z)
        self.og_l = local.take(W)
        self.out_s, self.out_r, self.out_l = send.take(4), recv.take(4), local.take(2)
        self.gg_s, self.gg_r = send.take(self.n_dev), recv.take(1)
        self.tmp_l = local.take(2 * S)
        self.n_send, self.n_recv, self.n_local = send.size, recv.size, local.size


def block_kernel(
    p,
    tok, cot, gin, cosr, sinr, posq, ids, wi0, wi1, wi2, wi3, wi4,
    block_out, in_grad, gain_grad, og0, og1, og2, og3, og4, rb0, rb1, rb2, rb3, rb4,
    gbuf, swap, n1, n2, gg, ga, w0, w1, w2, w3, w4, qpad, gmpad, kvall, kvt, dkv, lse, ot, gmt, mixed,
    hid, dgate, dup, dq, dkvr, gqkv, bsend, brecv, zsend, zrecv, resid, outv, ggs, ggr, tmp,
    ssem, rsem, lsem,
):
    YH, Z, X, S, R = p.YH, p.Z, p.X, p.S, p.R
    H = p.half
    HALF = Z * H
    win = [wi0, wi1, wi2, wi3, wi4]
    w = [w0, w1, w2, w3, w4]
    og = [og0, og1, og2, og3, og4]
    rb = [rb0, rb1, rb2, rb3, rb4]
    yh, z, x, c, tp = (lax.axis_index(a) for a in AXES)
    sib = {"core": 1 - c}
    holder = c == tp
    other = c != tp
    ctx_of = lambda a, b, d, e: ((a * Z + b) * X + d) * 2 + e
    ctx_me = ctx_of(yh, z, x, c)
    s_me = (yh * X + x) * 2 + tp
    zplus = lambda d: mod(z + d, Z)
    zminus = lambda d: mod(z + (Z - d), Z)
    row_of = lambda i, m: pl.multiple_of(i * m, m)

    def rc(src, dst, si, ri, dev):
        return pltpu.make_async_remote_copy(
            src_ref=src, dst_ref=dst, send_sem=ssem.at[si], recv_sem=rsem.at[ri],
            device_id=dev, device_id_type=MESH,
        )

    def wait_recv(dst, ri):
        rc(dst, dst, 0, ri, sib).wait_recv()

    def wait_send(src, si):
        rc(src, src, si, 0, sib).wait_send()

    def lc(src, dst, li):
        return pltpu.make_async_copy(src, dst, lsem.at[li])

    deltas = [
        (a, b, d, e, f)
        for a in range(YH) for b in range(Z) for d in range(X) for e in range(2) for f in range(p.TP)
        if a + b + d + e + f
    ]

    def away(a, b, d, e, f):
        return {
            "yh": mod(yh + a, YH), "z": mod(z + b, Z), "x": mod(x + d, X),
            "core": mod(c + e, 2), "tp": mod(tp + f, p.TP),
        }

    barrier = pltpu.get_barrier_semaphore()
    for delta in deltas:
        pl.semaphore_signal(barrier, inc=1, device_id=away(*delta), device_id_type=MESH)
    pl.semaphore_wait(barrier, len(deltas))

    gain_peers = [d for d in deltas if d[4] == 0]
    gbuf[ctx_me] = gin[...]
    for n, delta in enumerate(gain_peers):
        rc(gin, gbuf.at[ctx_me], p.gain_s + n, p.gain_r, away(*delta)).start()
    for n, src in enumerate((tok, cot)):
        rc(src.at[pl.ds(row_of(1 - c, H), H)], swap.at[n], p.swap_s + n, p.swap_r + n, sib).start()

    def seg(a, b, d):
        return pl.ds(pl.multiple_of(ctx_of(a, b, d, 0) * R, 2 * R), 2 * R)

    def block(a, b, d, e):
        return pl.ds(pl.multiple_of(ctx_of(a, b, d, e) * R, R), R)

    def piece(i, zz):
        if i == 0:
            return win[0].at[zz]
        n = p.cols[i]
        return win[i].at[:, pl.ds(pl.multiple_of(zz * n, n), n)]

    def w_stage1(i):
        dst = w[i].at[block(yh, z, x, c)]
        for d in range(Z):
            src = piece(i, zplus(d))
            si, ri = p.s1_s + i * Z + d, p.s1_r + (i * Z + d) * 2 + c
            if d == 0:
                @pl.when(holder)
                def _():
                    lc(src, dst, p.s1_l + i).start()

                @pl.when(other)
                def _():
                    rc(src, dst, si, ri, {"core": tp}).start()
            else:
                rc(src, dst, si, ri, {"z": zplus(d), "core": tp}).start()

    def w_stage1_sent(i):
        for d in range(Z):
            src = piece(i, zplus(d))
            if d == 0:
                @pl.when(other)
                def _():
                    wait_send(src, p.s1_s + i * Z + d)
            else:
                wait_send(src, p.s1_s + i * Z + d)

    plane = [(a, d, f) for a in range(YH) for d in range(X) for f in range(2) if a + d + f]

    def w_forward(i):
        @pl.when(holder)
        def _():
            for d in range(Z):
                zs = zminus(d)
                if d == 0:
                    lc(piece(i, z), w[i].at[block(yh, z, x, c)], p.s1_l + i).wait()
                    wait_recv(w[i].at[block(yh, z, x, 1 - c)], p.s1_r + i * Z * 2 + 1 - c)
                else:
                    for e in range(2):
                        wait_recv(w[i].at[block(yh, zs, x, e)], p.s1_r + (i * Z + d) * 2 + e)
                part = w[i].at[seg(yh, zs, x)]
                for n, (a, dx, f) in enumerate(plane):
                    rc(
                        part, part, p.s2_s + (i * Z + d) * S + n,
                        p.s2_r + (i * YH * X + a * X + dx) * Z + d, away(a, 0, dx, 0, f),
                    ).start()

    def w_wait(i):
        for a in range(YH):
            for dx in range(X):
                def wait_one():
                    for d in range(Z):
                        part = w[i].at[seg(mod(yh + YH - a, YH), zminus(d), mod(x + X - dx, X))]
                        wait_recv(part, p.s2_r + (i * YH * X + a * X + dx) * Z + d)
                if a + dx:
                    wait_one()
                else:
                    pl.when(other)(wait_one)

    def w_forward_sent(i):
        @pl.when(holder)
        def _():
            for d in range(Z):
                for n in range(len(plane)):
                    wait_send(w[i].at[seg(yh, zminus(d), x)], p.s2_s + (i * Z + d) * S + n)

    def rows_at(e, b):
        return pl.ds(pl.multiple_of((e * Z + b) * H, H), H)

    def ag_start(k, buf):
        mine = buf.at[rows_at(c, z)]
        base = k * 2 * Z
        for d in range(1, Z):
            rc(mine, mine, p.ag_s + base + d, p.ag_r + base + d, {"z": zplus(d)}).start()
        rc(mine, mine, p.ag_s + base, p.ag_r + base, sib).start()

    def ag_finish(k, buf):
        base = k * 2 * Z
        for d in range(1, Z):
            part = buf.at[rows_at(c, zminus(d))]
            wait_recv(part, p.ag_r + base + d)
            rc(part, part, p.ag_s + base + Z + d, p.ag_r + base + Z + d, sib).start()
        wait_recv(buf.at[rows_at(1 - c, z)], p.ag_r + base)
        for d in range(1, Z):
            wait_recv(buf.at[rows_at(1 - c, zminus(d))], p.ag_r + base + Z + d)

    def ag_sent(k, buf):
        base = k * 2 * Z
        for d in range(Z):
            wait_send(buf.at[rows_at(c, z)], p.ag_s + base + d)
        for d in range(1, Z):
            wait_send(buf.at[rows_at(c, zminus(d))], p.ag_s + base + Z + d)

    CW = p.model // CHUNKS

    def rs_start(k, terms):
        u = k % 2
        theirs = pl.ds(pl.multiple_of((1 - c) * HALF, HALF), HALF)
        own = pl.ds(pl.multiple_of(c * HALF, HALF), HALF)

        def product(j, rows):
            cols = pl.ds(pl.multiple_of(j * CW, CW), CW)
            total = None
            for a, b in terms:
                part = dot(a[rows, :], b[cols, :], NT)
                total = part if total is None else total + part
            return total

        def first(j, carry):
            value = product(j, theirs).astype(BF16)
            if k:
                wait_send(bsend.at[j], p.rb_s + (k - 1) * CHUNKS + j)
            bsend[j] = value
            rc(bsend.at[j], brecv.at[k, j], p.rb_s + k * CHUNKS + j, p.rb_r + k * CHUNKS + j, sib).start()
            return carry

        lax.fori_loop(0, CHUNKS, first, 0)

        def second(j, carry):
            value = product(j, own)
            wait_recv(brecv.at[k, j], p.rb_r + k * CHUNKS + j)
            zsend[u, j] = (value + brecv[k, j].astype(F32)).astype(BF16)
            for d in range(1, Z):
                ix = (k * CHUNKS + j) * Z + d
                rc(
                    zsend.at[u, j, pl.ds(row_of(zplus(d), H), H)], zrecv.at[k, j, d - 1],
                    p.rz_s + ix, p.rz_r + ix, {"z": zplus(d)},
                ).start()
            return carry

        lax.fori_loop(0, CHUNKS, second, 0)

    def rs_finish(k):
        u = k % 2
        parts = []
        for j in range(CHUNKS):
            value = zsend[u, j, pl.ds(row_of(z, H), H), :].astype(F32)
            for d in range(1, Z):
                wait_recv(zrecv.at[k, j, d - 1], p.rz_r + (k * CHUNKS + j) * Z + d)
                value = value + zrecv[k, j, d - 1].astype(F32)
            parts.append(value)
        return jnp.concatenate(parts, axis=1)

    def rs_sent(k):
        u = k % 2

        for j in range(CHUNKS):
            if k == 3:
                wait_send(bsend.at[j], p.rb_s + k * CHUNKS + j)
            for d in range(1, Z):
                wait_send(zsend.at[u, j, pl.ds(0, H)], p.rz_s + (k * CHUNKS + j) * Z + d)

    def dw_send(i, rows_ref, grad):
        per = 256 // (2 * R)

        def one(t, carry):
            cols = pl.ds(pl.multiple_of(t * 256, 256), 256)
            w[i][cols, :] = dot(rows_ref[:, cols], grad[...], TN).astype(BF16)
            for n in range(per):
                g = t * per + n
                xd, zd, yd = mod(g, X), mod(lax.div(g, jnp.int32(X)), Z), lax.div(g, jnp.int32(X * Z))
                mine = (xd == x) & (yd == yh) & holder

                @pl.when(jnp.logical_not(mine))
                def _():
                    rc(
                        w[i].at[pl.ds(pl.multiple_of(g * 2 * R, 2 * R), 2 * R)], rb[i].at[s_me, zd],
                        p.dw_s + i * p.nseg + g, p.dw_r + (i * S + s_me) * Z + zd,
                        {"yh": yd, "x": xd, "tp": c},
                    ).start()
            return carry

        lax.fori_loop(0, p.model // 256, one, 0)

    def dw_sent(i):
        for g in range(p.nseg):
            mine = (g % X == x) & (g // (X * Z) == yh) & holder

            @pl.when(jnp.logical_not(mine))
            def _():
                wait_send(w[i].at[pl.ds(g * 2 * R, 2 * R)], p.dw_s + i * p.nseg + g)

    def dw_reduce(i):
        n = p.cols[i]
        items = [(zd, at, min(TMP, n - at)) for zd in range(Z) for at in range(0, n, TMP)]

        def loads(q):
            zd, at, width = items[q]
            return [
                lc(
                    rb[i].at[mod(s_me + d, S), zd, :, pl.ds(at, width)],
                    tmp.at[q % 2, d - 1, :, pl.ds(0, width)], p.tmp_l + q % 2 * S + d,
                )
                for d in range(1, S)
            ]

        def begin(q):
            zd, at, _ = items[q]
            if at == 0:
                for d in range(1, S):
                    s = mod(s_me + d, S)
                    wait_recv(rb[i].at[s, zd], p.dw_r + (i * S + s) * Z + zd)
            for copy in loads(q):
                copy.start()

        @pl.when(holder)
        def _():
            begin(0)
            for q, (zd, at, width) in enumerate(items):
                if q + 1 < len(items):
                    begin(q + 1)
                for copy in loads(q):
                    copy.wait()
                mine = seg(yh, zd, x)
                total = w[i][mine, at : at + width].astype(F32)
                for d in range(1, S):
                    total = total + tmp[q % 2, d - 1, :, 0:width].astype(F32)
                w[i][mine, at : at + width] = total.astype(BF16)
                if at + width < n:
                    continue
                for e in range(2):
                    src = w[i].at[block(yh, zd, x, e)]
                    here = (z == zd) & (c == e)

                    @pl.when(here)
                    def _():
                        lc(src, og[i].at[z], p.og_l + i).start()

                    @pl.when(jnp.logical_not(here))
                    def _():
                        rc(
                            src, og[i].at[z], p.og_s + (i * Z + zd) * 2 + e, p.og_r + i * Z + z,
                            {"z": jnp.int32(zd), "core": jnp.int32(e)},
                        ).start()

    def dw_done(i):
        for b in range(Z):
            here = (z == b) & holder

            @pl.when(here)
            def _():
                lc(w[i].at[block(yh, z, x, c)], og[i].at[z], p.og_l + i).wait()

            @pl.when(jnp.logical_not(here))
            def _():
                wait_recv(og[i].at[b], p.og_r + i * Z + b)

        @pl.when(holder)
        def _():
            for zd in range(Z):
                for e in range(2):
                    @pl.when(jnp.logical_not((z == zd) & (c == e)))
                    def _():
                        wait_send(w[i].at[block(yh, zd, x, e)], p.og_s + (i * Z + zd) * 2 + e)

    def deliver(k, out):
        dst = out.at[pl.ds(row_of(c, H), H)]
        for t in range(p.TP):
            here = holder & (tp == t)

            @pl.when(here)
            def _():
                lc(outv.at[k], dst, p.out_l + k).start()

            @pl.when(jnp.logical_not(here))
            def _():
                rc(outv.at[k], dst, p.out_s + k * 2 + t, p.out_r + k * 2 + c, {"core": tp, "tp": jnp.int32(t)}).start()

    def delivered(k, out):
        for e in range(2):
            here = holder & (c == e)

            @pl.when(here)
            def _():
                lc(outv.at[k], out.at[pl.ds(row_of(c, H), H)], p.out_l + k).wait()

            @pl.when(jnp.logical_not(here))
            def _():
                wait_recv(out.at[pl.ds(e * H, H)], p.out_r + k * 2 + e)
        for t in range(p.TP):
            @pl.when(jnp.logical_not(holder & (tp == t)))
            def _():
                wait_send(outv.at[k], p.out_s + k * 2 + t)

    w_stage1(0)
    for n in range(2):
        wait_recv(swap.at[n], p.swap_r + n)
    mine = pl.ds(row_of(c, H), H)
    token_rows = jnp.where(holder, tok[mine, :].astype(F32), swap[0].astype(F32))
    grad_rows = jnp.where(holder, cot[mine, :].astype(F32), swap[1].astype(F32))
    gg[rows_at(c, z), :] = grad_rows.astype(BF16)
    factor_attn = lax.rsqrt(jnp.mean(token_rows * token_rows, axis=1, keepdims=True) + EPS)
    scaled_attn = token_rows * factor_attn
    wait_recv(gbuf.at[pl.ds(0, p.n_ctx - 1)], p.gain_r)
    q = p.n_ctx * 128 // p.model
    gain_parts = []
    for b in range(p.model // 128):
        total = gbuf[b * q]
        for n in range(1, q):
            total = total + gbuf[b * q + n]
        gain_parts.append(total)
    gains = jnp.concatenate(gain_parts, axis=1)
    gain_attn, gain_mlp = gains[0:1, :], gains[1:2, :]
    n1[rows_at(c, z), :] = (scaled_attn * gain_attn).astype(BF16)
    ag_start(0, n1)
    w_forward(0)
    w_stage1(1)
    ag_finish(0, n1)
    ag_start(1, gg)
    for i in (2, 3, 4):
        w_stage1(i)
    w_wait(0)

    lane = lax.broadcasted_iota(jnp.int32, (1, 128), 1)
    low = lane < HEAD_DIM
    first_half = mod(lane, HEAD_DIM) < HEAD_DIM // 2

    def rotate(t, cosine, sine):
        turned = jnp.where(first_half, pltpu.roll(t, 96, 1), pltpu.roll(t, 32, 1))
        return t * cosine + turned * sine

    lin = dot(n1[...], w0[...], NN)
    cosine, sine = cosr[...], sinr[...]
    scale = HEAD_DIM ** (-0.5)
    pairs = p.qc // 128
    for n in range(pairs):
        turned_q = rotate(lin[:, n * 128 : (n + 1) * 128], cosine, sine).astype(BF16).astype(F32) * scale
        qpad[2 * n] = jnp.where(low, turned_q, 0.0).astype(BF16)
        qpad[2 * n + 1] = jnp.where(low, pltpu.roll(turned_q, 64, 1), 0.0).astype(BF16)
    kv_lin = lin[:, p.qc : p.qc + 128]
    own_rows = pl.ds(pl.multiple_of(s_me * p.rows, p.rows), p.rows)
    kvall[own_rows, :] = jnp.where(low, rotate(kv_lin, cosine, sine), kv_lin).astype(BF16)
    for n, (a, dx, f) in enumerate(plane):
        rc(kvall.at[own_rows], kvall.at[own_rows], p.kv_s + n, p.kv_r + n, away(a, 0, dx, 0, f)).start()

    def from_plane(a, dx, f):
        s = (mod(yh + YH - a, YH) * X + mod(x + X - dx, X)) * 2 + mod(tp + 2 - f, 2)
        return pl.ds(pl.multiple_of(s * p.rows, p.rows), p.rows)

    for n, delta in enumerate(plane):
        wait_recv(kvall.at[from_plane(*delta)], p.kv_r + n)
    eye = (
        lax.broadcasted_iota(jnp.int32, (128, 128), 0) == lax.broadcasted_iota(jnp.int32, (128, 128), 1)
    ).astype(BF16)
    kvt[...] = dot(eye, kvall[...], NT).astype(BF16)

    T = p.tile
    KC = p.rows
    down = lax.broadcasted_iota(jnp.int32, (BLOCK, 1), 0)

    def masked(s, rows, scores):
        at = posq[:, rows]
        parts = []
        for b in range(2 * Z):
            allowed = down <= at - ids[s, b] * BLOCK
            parts.append(jnp.where(allowed, scores[b * BLOCK : (b + 1) * BLOCK, :], NEG))
        return jnp.concatenate(parts, axis=0)

    def keys(s):
        return pl.ds(s * KC, KC)

    for n in range(pairs):
        def attend(t, carry):
            rows = pl.ds(pl.multiple_of(t * T, T), T)
            outs = []
            for e in range(2):
                h = 2 * n + e
                query = qpad[h, rows, :]
                top = jnp.full((8, T), NEG, F32)
                for s in range(S):
                    scores = masked(s, rows, dot(kvall[keys(s), :], query, NT))
                    dkv[keys(s), :] = scores
                    top = jnp.maximum(top, jnp.max(scores.reshape(KC // 8, 8, T), axis=0))
                top = jnp.max(top, axis=0, keepdims=True)
                total = jnp.zeros((8, T), F32)
                for s in range(S):
                    grown = jnp.exp(dkv[keys(s), :] - top)
                    dkv[keys(s), :] = grown
                    total = total + jnp.sum(grown.reshape(KC // 8, 8, T), axis=0)
                total = jnp.sum(total, axis=0, keepdims=True)
                lse[h : h + 1, rows] = top + jnp.log(total)
                share = 1.0 / total
                out = jnp.zeros((128, T), F32)
                for s in range(S):
                    out = out + dot(kvt[:, keys(s)], (dkv[keys(s), :] * share).astype(BF16), NN)
                outs.append(out[HEAD_DIM:, :])
            out = jnp.concatenate(outs, axis=0)
            ot[n, :, rows] = out
            mixed[rows, n * 128 : (n + 1) * 128] = jnp.transpose(out).astype(BF16)
            return carry

        lax.fori_loop(0, p.rows // T, attend, 0)
        if n == 0:
            w_forward(1)
            w_forward(2)
    w_forward(3)
    w_forward(4)
    w_wait(1)
    rs_start(0, [(mixed, w1)])
    ag_finish(1, gg)
    residual = token_rows + rs_finish(0)
    resid[...] = residual
    factor_mlp = lax.rsqrt(jnp.mean(residual * residual, axis=1, keepdims=True) + EPS)
    scaled_mlp = residual * factor_mlp
    n2[rows_at(c, z), :] = (scaled_mlp * gain_mlp).astype(BF16)
    ag_start(2, n2)
    for i in (2, 3, 4):
        w_wait(i)
    ag_finish(2, n2)

    def feed(t, carry):
        cols = pl.ds(pl.multiple_of(t * 256, 256), 256)
        gate = dot(n2[...], w2[:, cols], NN)
        up = dot(n2[...], w3[:, cols], NN)
        back = dot(gg[...], w4[:, cols], NN)
        sig = jax.nn.sigmoid(gate)
        silu = gate * sig
        hid[:, cols] = (silu * up).astype(BF16)
        dgate[:, cols] = (back * up * sig * (1.0 + gate * (1.0 - sig))).astype(BF16)
        dup[:, cols] = (back * silu).astype(BF16)
        return carry

    lax.fori_loop(0, p.fc // 256, feed, 0)
    rs_start(1, [(dgate, w2), (dup, w3)])
    rs_sent(0)
    rs_start(2, [(hid, w4)])
    w_forward_sent(4)
    dw_send(4, gg, hid)
    grad_norm_mlp = rs_finish(1)
    weighted = grad_norm_mlp * gain_mlp
    u = resid[...] * factor_mlp
    grad_residual = grad_rows + factor_mlp * (weighted - u * jnp.mean(weighted * u, axis=1, keepdims=True))
    gain_mlp_part = jnp.sum(grad_norm_mlp * u, axis=0, keepdims=True)
    ga[rows_at(c, z), :] = grad_residual.astype(BF16)
    ag_start(3, ga)
    w_forward_sent(2)
    dw_send(2, n2, dgate)
    w_forward_sent(3)
    dw_send(3, n2, dup)
    outv[0] = (resid[...] + rs_finish(2)).astype(BF16)
    resid[...] = grad_residual
    deliver(0, block_out)
    ag_finish(3, ga)

    for n in range(pairs):
        gm = dot(ga[...], w1[:, n * 128 : (n + 1) * 128], NN).astype(BF16).astype(F32)
        gmt[n] = jnp.transpose(gm)
        gmpad[2 * n] = jnp.where(low, 0.0, pltpu.roll(gm, 64, 1)).astype(BF16)
        gmpad[2 * n + 1] = jnp.where(low, 0.0, gm).astype(BF16)
    w_forward_sent(1)
    dw_send(1, ga, mixed)
    dkv[:, 0:128] = jnp.zeros((p.seq, 128), F32)
    for n in range(pairs):
        def attend_back(t, carry):
            rows = pl.ds(pl.multiple_of(t * T, T), T)
            agree = ot[n, :, rows] * gmt[n, :, rows]
            outs = []
            for e in range(2):
                h = 2 * n + e
                query, back = qpad[h, rows, :], gmpad[h, rows, :]
                level = lse[h : h + 1, rows]
                delta = jnp.sum(agree[e * HEAD_DIM : (e + 1) * HEAD_DIM, :], axis=0, keepdims=True)
                out = jnp.zeros((128, T), F32)
                for s in range(S):
                    here = kvall[keys(s), :]
                    probs = jnp.exp(masked(s, rows, dot(here, query, NT)) - level)
                    ds = (probs * (dot(here, back, NT) - delta)).astype(BF16)
                    out = out + dot(kvt[:, keys(s)], ds, NN)
                    dkv[keys(s), 0:128] += dot(ds, query, NN) + dot(probs.astype(BF16), back, NN)
                outs.append(out[:HEAD_DIM, :])
            dq[rows, n * 128 : (n + 1) * 128] = jnp.transpose(jnp.concatenate(outs, axis=0)) * scale
            return carry

        lax.fori_loop(0, p.rows // T, attend_back, 0)
    for n, (a, dx, f) in enumerate(plane):
        s = (mod(yh + a, YH) * X + mod(x + dx, X)) * 2 + mod(tp + f, 2)
        rc(
            dkv.at[pl.ds(pl.multiple_of(s * p.rows, p.rows), p.rows), pl.ds(0, 128)], dkvr.at[n],
            p.dkv_s + n, p.dkv_r + n, away(a, 0, dx, 0, f),
        ).start()
    for n in range(pairs):
        cols = slice(n * 128, (n + 1) * 128)
        gqkv[:, cols] = rotate(dq[:, cols], cosine, -sine).astype(BF16)
    dw_reduce(4)
    dw_reduce(2)
    dkv_own = dkv[own_rows, 0:128]
    for n in range(len(plane)):
        wait_recv(dkvr.at[n], p.dkv_r + n)
        dkv_own = dkv_own + dkvr[n]
    gqkv[:, p.qc : p.qc + 128] = jnp.where(low, rotate(dkv_own, cosine, -sine), dkv_own).astype(BF16)
    rs_sent(1)
    rs_start(3, [(gqkv, w0)])
    w_forward_sent(0)
    dw_send(0, n1, gqkv)
    dw_reduce(3)
    dw_reduce(1)
    grad_norm_attn = rs_finish(3)
    weighted = grad_norm_attn * gain_attn
    outv[1] = (
        resid[...] + factor_attn * (weighted - scaled_attn * jnp.mean(weighted * scaled_attn, axis=1, keepdims=True))
    ).astype(BF16)
    deliver(1, in_grad)

    gain_attn_part = jnp.sum(grad_norm_attn * scaled_attn, axis=0, keepdims=True)
    both_gains = jnp.concatenate([gain_attn_part, gain_mlp_part, jnp.zeros((6, p.model), F32)], axis=0)
    for b in range(p.model // 128):
        ggs[b] = both_gains[:, b * 128 : (b + 1) * 128]
    dev_me = ctx_me * p.TP + tp
    ggr[dev_me] = ggs[lax.div(ctx_me * R, jnp.int32(128))]
    for n, delta in enumerate(deltas):
        to = away(*delta)
        there = ctx_of(to["yh"], to["z"], to["x"], to["core"])
        rc(ggs.at[lax.div(there * R, jnp.int32(128))], ggr.at[dev_me], p.gg_s + n, p.gg_r, to).start()

    dw_reduce(0)
    wait_recv(ggr.at[pl.ds(0, p.n_dev - 1)], p.gg_r)
    total = ggr[0]
    for n in range(1, p.n_dev):
        total = total + ggr[n]
    gain_grad[...] = total

    for i in range(5):
        dw_done(i)
        dw_sent(i)
        w_stage1_sent(i)
    for k, buf in enumerate((n1, gg, n2, ga)):
        ag_sent(k, buf)
    rs_sent(2)
    rs_sent(3)
    delivered(0, block_out)
    delivered(1, in_grad)
    for n in range(len(plane)):
        wait_send(kvall.at[own_rows], p.kv_s + n)
        wait_send(dkvr.at[n], p.dkv_s + n)
    for n in range(len(gain_peers)):
        wait_send(gin, p.gain_s + n)
    for n in range(len(deltas)):
        wait_send(ggs.at[0], p.gg_s + n)
    for n in range(2):
        wait_send(swap.at[n], p.swap_s + n)


def local(sizes, tokens, block_ids, gain_attn, w_query, key_weight, value_weight, w_out, gain_mlp,
          w_gate, w_up, w_down, cotangent):
    row_count, model = tokens.shape
    p = Plan(sizes, model, w_query.shape[1], key_weight.shape[1], w_gate.shape[1], row_count)
    YH, Z, X, S, R = p.YH, p.Z, p.X, p.S, p.R
    yh, z, x, c, tp = (lax.axis_index(a) for a in AXES)
    ctx_me = ((yh * Z + z) * X + x) * 2 + c
    s_me = (yh * X + x) * 2 + tp
    ids = block_ids.reshape(YH, Z, X, 2, 2).transpose(0, 2, 3, 4, 1).reshape(S, 2 * Z)
    positions = (ids[:, :, None] * BLOCK + jnp.arange(BLOCK, dtype=jnp.int32)).reshape(S, p.rows)
    own = lax.dynamic_slice_in_dim(positions, s_me, 1, 0)
    half = HEAD_DIM // 2
    frequencies = THETA ** (-(jnp.arange(half, dtype=F32) * 2.0 / HEAD_DIM))
    angles = own.reshape(p.rows, 1).astype(F32) * jnp.tile(frequencies, 4)[None, :]
    signs = jnp.where(jnp.arange(128) % HEAD_DIM < half, -1.0, 1.0).astype(F32)
    cosine, sine = jnp.cos(angles), jnp.sin(angles) * signs
    gains = jnp.stack([gain_attn, gain_mlp]).astype(F32)
    gin = lax.dynamic_update_slice(jnp.zeros((8, 128), F32), gains, (0, lax.rem(ctx_me * R, 128)))
    packed = jnp.concatenate(
        [w_query.reshape(R, Z, p.qc), key_weight.reshape(R, Z, p.kc), value_weight.reshape(R, Z, p.kc)], axis=2
    ).transpose(1, 0, 2)

    V = pl.BlockSpec(memory_space=pltpu.VMEM)
    A = pl.BlockSpec(memory_space=pl.ANY)
    H = p.half
    sd = jax.ShapeDtypeStruct
    out_shape = [sd((row_count, model), BF16), sd((row_count, model), BF16), sd((8, 128), F32)]
    out_shape += [sd((Z, R, n), BF16) for n in p.cols]
    out_shape += [sd((S, Z, 2 * R, n), BF16) for n in p.cols]
    CW = model // CHUNKS
    scratch = [
        pltpu.VMEM((p.n_ctx, 8, 128), F32),
        pltpu.VMEM((2, H, model), BF16),
        *[pltpu.VMEM((p.rows, model), BF16) for _ in range(4)],
        *[pltpu.VMEM((model, n), BF16) for n in p.cols],
        pltpu.VMEM((p.qc // 64, p.rows, 128), BF16),
        pltpu.VMEM((p.qc // 64, p.rows, 128), BF16),
        pltpu.VMEM((p.seq, 128), BF16),
        pltpu.VMEM((128, p.seq), BF16),
        pltpu.VMEM((p.seq, p.tile), F32),
        pltpu.VMEM((8, p.rows), F32),
        pltpu.VMEM((p.qc // 128, 128, p.rows), F32),
        pltpu.VMEM((p.qc // 128, 128, p.rows), F32),
        pltpu.VMEM((p.rows, p.qc), BF16),
        *[pltpu.VMEM((p.rows, p.fc), BF16) for _ in range(3)],
        pltpu.VMEM((p.rows, p.qc), F32),
        pltpu.VMEM((S - 1, p.rows, 128), F32),
        pltpu.VMEM((p.rows, p.cols[0]), BF16),
        pltpu.VMEM((CHUNKS, Z * H, CW), BF16),
        pltpu.VMEM((4, CHUNKS, Z * H, CW), BF16),
        pltpu.VMEM((2, CHUNKS, Z * H, CW), BF16),
        pltpu.VMEM((4, CHUNKS, Z - 1, H, CW), BF16),
        pltpu.VMEM((H, model), F32),
        pltpu.VMEM((2, H, model), BF16),
        pltpu.VMEM((model // 128, 8, 128), F32),
        pltpu.VMEM((p.n_dev, 8, 128), F32),
        pltpu.VMEM((2, S - 1, 2 * R, TMP), BF16),
        pltpu.SemaphoreType.DMA((p.n_send,)),
        pltpu.SemaphoreType.DMA((p.n_recv,)),
        pltpu.SemaphoreType.DMA((p.n_local,)),
    ]
    outs = pl.pallas_call(
        lambda *refs: block_kernel(p, *refs),
        out_shape=out_shape,
        in_specs=[V] * 6 + [pl.BlockSpec(memory_space=pltpu.SMEM)] + [A] * 5,
        out_specs=[A, A, V] + [A] * 10,
        scratch_shapes=scratch,
        compiler_params=pltpu.CompilerParams(
            collective_id=0, has_side_effects=True, vmem_limit_bytes=64000 * 1024
        ),
        name="block",
    )(
        tokens, cotangent, gin, cosine, sine, own, ids,
        packed, w_out, w_gate, w_up, w_down,
    )
    block_out, in_grad, gain_grad = outs[:3]
    g_qkv, g_out, g_gate, g_up, g_down = (
        g.transpose(1, 0, 2).astype(F32) for g in outs[3:8]
    )
    gain_grads = lax.dynamic_slice(gain_grad, (0, lax.rem(ctx_me * R, 128)), (2, R))
    return (
        block_out,
        in_grad,
        gain_grads[0],
        g_qkv[:, :, : p.qc].reshape(R, -1),
        g_qkv[:, :, p.qc : p.qc + p.kc].reshape(R, -1),
        g_qkv[:, :, p.qc + p.kc :].reshape(R, -1),
        g_out.reshape(R, -1),
        gain_grads[1],
        g_gate.reshape(R, -1),
        g_up.reshape(R, -1),
        g_down.reshape(R, -1),
    )


def solution(mesh):
    n_ctx, tp = mesh.devices.shape
    Z = 4
    X = 2 if n_ctx == 16 else 4
    YH = n_ctx // (Z * X * 2)
    sizes = (YH, Z, X, tp)
    split = Mesh(mesh.devices.reshape(YH, Z, X, 2, tp), AXES)
    ctx = AXES[:4]
    rows, weight, vector = P(ctx, None), P(ctx, "tp"), P(ctx)
    return jax.shard_map(
        lambda *args: local(sizes, *args),
        mesh=split,
        in_specs=(rows, P(), vector, weight, weight, weight, weight, vector, weight, weight, weight, rows),
        out_specs=(rows, rows, vector, weight, weight, weight, weight, vector, weight, weight, weight),
        check_vma=False,
    )
```

```python
import math

import jax
import jax.numpy as jnp
from jax import lax
from jax.experimental import pallas as pl
from jax.experimental.pallas import tpu as pltpu
from jax.sharding import Mesh
from jax.sharding import PartitionSpec as P

HEAD_DIM = 64
BLOCK = 64
EPS = 1e-05
THETA = 500000.0
NEG = -1e30
MESH = pl.DeviceIdType.MESH
AXES = ("yh", "z", "x", "core", "tp")
NN = (((1,), (0,)), ((), ()))
NT = (((1,), (1,)), ((), ()))
TN = (((0,), (0,)), ((), ()))
F32 = jnp.float32
BF16 = jnp.bfloat16
CHUNKS = 4
TMP = 128
WIDE = (2, 3, 4)
ALL = (0, 1, 2, 3)
FILL = {
    "inputs": [("stage", 1, ALL)],
    "n1_0": [("stage", 2, ALL)],
    "n1_3": [("cotangent", 0), ("stage", 3, ALL)],
    "kv": [("forward", 1, ALL)],
    "attend_0": [("cotangent", 1)],
    "attend_1": [("cotangent", 2), ("forward", 2, ALL), ("stage", 4, ALL)],
    "attend_2": [("cotangent", 3), ("forward", 3, ALL)],
    "n2_2": [("forward", 4, ALL)],
    "norm_0": [("reduce", 4, (0,))],
    "norm_1": [("reduce", 4, (1,))],
    "norm_2": [("reduce", 4, (2,))],
    "norm_3": [("reduce", 4, (3,))],
    "ga_0": [("sum", (0, 1))],
    "ga_1": [("sum", (2, 3))],
    "ga_3": [("reduce", 2, (0, 1))],
    "back_0": [("reduce", 2, (2, 3))],
    "back_1": [("reduce", 3, (0, 1))],
    "back_2": [("reduce", 3, (2, 3))],
    "terms": [("reduce", 1, ALL)],
    "end_1": [("reduce", 0, ALL)],
}


def dot(a, b, dims):
    return lax.dot_general(a, b, dims, preferred_element_type=F32)


def mod(a, n):
    return lax.rem(a, jnp.int32(n))


class Sems:
    def __init__(self):
        self.size = 0

    def take(self, count):
        first = self.size
        self.size += count
        return first


class Plan:
    def __init__(self, sizes, model, heads_cols, kv_cols, hidden_cols, tokens):
        self.YH, self.Z, self.X, self.TP = sizes
        self.n_ctx = self.YH * self.Z * self.X * 2
        self.n_dev = self.n_ctx * self.TP
        self.S = self.YH * self.X * 2
        self.YX = self.YH * self.X
        self.R = model // self.n_ctx
        self.model = model
        self.qc = heads_cols // self.Z
        self.kc = kv_cols // self.Z
        self.fc = hidden_cols // (2 * self.Z)
        self.cols = [self.qc + 2 * self.kc, self.qc, self.fc, self.fc, self.fc]
        self.half = tokens // 2
        self.rows = 2 * self.Z * self.half
        self.wide_rows = 2 * self.rows
        self.seq = self.S * self.rows
        self.nseg = self.n_ctx // 2
        self.tile = 256 if self.seq <= 2048 else 128
        send, recv, local = Sems(), Sems(), Sems()
        W, Z, S, YX = 5, self.Z, self.S, self.YX
        self.gain_s, self.gain_r = send.take(self.n_ctx), recv.take(1)
        self.swap_s, self.swap_r = send.take(2), recv.take(2)
        self.s1_s, self.s1_r, self.s1_l = send.take(W * Z * 2), recv.take(W * Z * 2), local.take(W)
        self.s2_s, self.s2_r = send.take(W * Z * S), recv.take(W * YX * Z)
        self.ag_s, self.ag_r = send.take(4 * 5 * Z), recv.take(4 * 4 * Z)
        self.rb_s, self.rb_r = send.take(4 * CHUNKS), recv.take(4 * CHUNKS)
        self.ry_s, self.ry_r = send.take(4 * CHUNKS), recv.take(4 * CHUNKS)
        self.rz_s, self.rz_r = send.take(4 * CHUNKS * Z), recv.take(4 * CHUNKS * (Z + 1))
        self.kv_s, self.kv_r = send.take(S), recv.take(S)
        self.dkv_s, self.dkv_r = send.take(S), recv.take(S)
        self.dw_s, self.dw_r = send.take(W * self.nseg), recv.take(W * S * Z)
        self.og_s, self.og_r = send.take(W * Z * 2), recv.take(W * Z * 2)
        self.og_l = local.take(W)
        self.out_s, self.out_r, self.out_l = send.take(4), recv.take(4), local.take(2)
        self.gg_s, self.gg_r = send.take(self.n_dev), recv.take(1)
        self.tmp_l = local.take(2 * S)
        self.pack_l = local.take(3)
        self.n_send, self.n_recv, self.n_local = send.size, recv.size, local.size


def block_kernel(
    p,
    tok, cot, gin, cosr, sinr, posq, ids, wq, wk, wv, wi1, wi2, wi3, wi4,
    block_out, in_grad, gain_grad, og0, og1, og2, og3, og4, rb0, rb1, rb2, rb3, rb4,
    gbuf, swap, stq, stk, stv, pack, n1, n2, gg, ga, w0, w1, w2, w3, w4,
    qpad, gmpad, kvall, dkv, lse, ot, mixed, hid, dgate, dup, gate, up, dq, dkvr, gqkv,
    bsend, brecvs, ysend, yrecv, zsend, zrecv, acc, toks, resid, resid2, ggs, ggr, tmp,
    ssem, rsem, lsem,
):
    YH, Z, X, S, YX, R = p.YH, p.Z, p.X, p.S, p.YX, p.R
    H = p.half
    HALF = Z * H
    win = [None, wi1, wi2, wi3, wi4]
    w = [w0, w1, w2, w3, w4]
    og = [og0, og1, og2, og3, og4]
    rb = [rb0, rb1, rb2, rb3, rb4]
    yh, z, x, c, tp = (lax.axis_index(a) for a in AXES)
    sib = {"core": 1 - c}
    holder = c == tp
    other = c != tp
    ctx_of = lambda a, b, d, e: ((a * Z + b) * X + d) * 2 + e
    ctx_me = ctx_of(yh, z, x, c)
    s_me = (yh * X + x) * 2 + tp
    yx_me = yh * X + x
    zplus = lambda d: mod(z + d, Z)
    zminus = lambda d: mod(z + (Z - d), Z)
    row_of = lambda i, m: pl.multiple_of(i * m, m)
    pending = []

    def rc(src, dst, si, ri, dev):
        return pltpu.make_async_remote_copy(
            src_ref=src, dst_ref=dst, send_sem=ssem.at[si], recv_sem=rsem.at[ri],
            device_id=dev, device_id_type=MESH,
        )

    def wait_recv(dst, ri):
        rc(dst, dst, 0, ri, sib).wait_recv()

    def wait_send(src, si):
        rc(src, src, si, 0, sib).wait_send()

    def lc(src, dst, li):
        return pltpu.make_async_copy(src, dst, lsem.at[li])

    def when(pred, do):
        if pred is None:
            do()
        else:
            pl.when(pred)(do)

    def send(src, dst, si, ri, dev, pred=None):
        when(pred, lambda: rc(src, dst, si, ri, dev).start())
        pending.append(lambda: when(pred, lambda: wait_send(src, si)))

    loads = [lc(a, b, p.pack_l + n) for n, (a, b) in enumerate(((wq, stq), (wk, stk), (wv, stv)))]
    for copy in loads:
        copy.start()

    deltas = [
        (a, b, d, e, f)
        for a in range(YH) for b in range(Z) for d in range(X) for e in range(2) for f in range(p.TP)
        if a + b + d + e + f
    ]

    def away(a, b, d, e, f):
        return {
            "yh": mod(yh + a, YH), "z": mod(z + b, Z), "x": mod(x + d, X),
            "core": mod(c + e, 2), "tp": mod(tp + f, p.TP),
        }

    barrier = pltpu.get_barrier_semaphore()
    for delta in deltas:
        pl.semaphore_signal(barrier, inc=1, device_id=away(*delta), device_id_type=MESH)

    lane = lax.broadcasted_iota(jnp.int32, (1, 128), 1)
    low = lane < HEAD_DIM
    for copy in loads:
        copy.wait()
    for b in range(Z):
        pack[b, :, 0 : p.qc] = stq[:, b * p.qc : (b + 1) * p.qc]
        both = slice(b // 2 * 128, b // 2 * 128 + 128)
        key, val = stk[:, both].astype(F32), stv[:, both].astype(F32)
        if b % 2:
            pair = jnp.where(low, pltpu.roll(key, 64, 1), val)
        else:
            pair = jnp.where(low, key, pltpu.roll(val, 64, 1))
        pack[b, :, p.qc : p.qc + 128] = pair.astype(BF16)
    pl.semaphore_wait(barrier, len(deltas))

    gain_peers = [d for d in deltas if d[4] == 0]
    gbuf[ctx_me] = gin[...]
    for n, src in enumerate((tok, cot)):
        send(src.at[pl.ds(row_of(1 - c, H), H)], swap.at[n], p.swap_s + n, p.swap_r + n, sib)
    for n, delta in enumerate(gain_peers):
        send(gin, gbuf.at[ctx_me], p.gain_s + n, p.gain_r, away(*delta))

    def seg(a, b, d):
        return pl.ds(pl.multiple_of(ctx_of(a, b, d, 0) * R, 2 * R), 2 * R)

    def block(a, b, d, e):
        return pl.ds(pl.multiple_of(ctx_of(a, b, d, e) * R, R), R)

    def piece(i, zz, cc):
        if i == 0:
            return pack.at[zz]
        n = p.cols[i]
        return win[i].at[:, pl.ds(row_of(zz * 2 + cc if i in WIDE else zz, n), n)]

    def s1r(i, d, e):
        return p.s1_r + (i * Z + d) * 2 + e

    def w_stage1(i, steps=None):
        dst = w[i].at[block(yh, z, x, c)]
        for d in range(Z) if steps is None else steps:
            si = p.s1_s + (i * Z + d) * 2
            if i in WIDE:
                for e in range(2):
                    src = piece(i, zplus(d), mod(c + e, 2))
                    if d + e:
                        send(src, dst, si + e, s1r(i, d, c), {"z": zplus(d), "core": mod(c + e, 2)})
                    else:
                        lc(src, dst, p.s1_l + i).start()
                continue
            src = piece(i, zplus(d), c)
            if d == 0:
                pl.when(holder)(lambda: lc(src, dst, p.s1_l + i).start())
            send(src, dst, si, s1r(i, d, c), {"z": zplus(d), "core": tp}, other if d == 0 else None)

    plane = [(a, d, f) for a in range(YH) for d in range(X) for f in range(2) if a + d + f]
    line = [(a, d) for a in range(YH) for d in range(X) if a + d]

    def w_forward(i, steps=None):
        def arrived(d):
            zs = zminus(d)
            if d == 0:
                lc(piece(i, z, c), w[i].at[block(yh, z, x, c)], p.s1_l + i).wait()
                wait_recv(w[i].at[block(yh, z, x, 1 - c)], s1r(i, 0, 1 - c))
            else:
                for e in range(2):
                    wait_recv(w[i].at[block(yh, zs, x, e)], s1r(i, d, e))

        for d in range(Z) if steps is None else steps:
            when(None if i in WIDE else holder, lambda: arrived(d))
            part = w[i].at[seg(yh, zminus(d), x)]
            for n, peer in enumerate(line if i in WIDE else plane):
                send(
                    part, part, p.s2_s + (i * Z + d) * S + n,
                    p.s2_r + (i * YX + peer[0] * X + peer[1]) * Z + d,
                    away(peer[0], 0, peer[1], 0, 0 if i in WIDE else peer[2]),
                    None if i in WIDE else holder,
                )

    def w_wait(i):
        for a in range(YH):
            for dx in range(X):
                def wait_all():
                    for d in range(Z):
                        part = w[i].at[seg(mod(yh + YH - a, YH), zminus(d), mod(x + X - dx, X))]
                        wait_recv(part, p.s2_r + (i * YX + a * X + dx) * Z + d)
                if a + dx:
                    wait_all()
                elif i not in WIDE:
                    pl.when(other)(wait_all)

    def rows_at(g, e, b):
        return pl.ds(pl.multiple_of(((g * 2 + e) * Z + b) * H, H), H)

    up_z, down_z = jnp.minimum(z + 1, Z - 1), jnp.maximum(z - 1, 0)

    def ag_step(k, buf, dist, wide):
        g = tp if wide else 0
        rbase, sbase = p.ag_r + k * 4 * Z, p.ag_s + k * 5 * Z
        if dist == 0:
            mine = buf.at[rows_at(g, c, z)]
            send(mine, mine, sbase + z, rbase + z, {"z": up_z}, z < Z - 1)
            send(mine, mine, sbase + 4 * Z + z, rbase + z, {"z": down_z}, z > 0)
            send(mine, mine, sbase + Z + z, rbase + Z + z, sib)
            if wide:
                send(mine, mine, sbase + 2 * Z + z, rbase + 2 * Z + z, {"tp": 1 - tp})
            return
        for sign in (-1, 1):
            there = z + sign * dist
            has = (there >= 0) & (there < Z)
            b = jnp.clip(there, 0, Z - 1)
            part = buf.at[rows_at(g, c, b)]
            pl.when(has)(lambda: wait_recv(part, rbase + b))
            if dist < Z - 1:
                if sign < 0:
                    send(part, part, sbase + b, rbase + b, {"z": up_z}, has & (z < Z - 1))
                else:
                    send(part, part, sbase + b, rbase + b, {"z": down_z}, has & (z > 0))
            send(part, part, sbase + Z + b, rbase + Z + b, sib, has)
            if wide:
                send(part, part, sbase + 2 * Z + b, rbase + 2 * Z + b, {"tp": 1 - tp}, has)

    def ag_tail(k, buf, wide):
        g = tp if wide else 0
        rbase, sbase = p.ag_r + k * 4 * Z, p.ag_s + k * 5 * Z
        for b in range(Z):
            wait_recv(buf.at[rows_at(g, 1 - c, b)], rbase + Z + b)
        if not wide:
            return
        for b in range(Z):
            part = buf.at[rows_at(1 - tp, c, b)]
            wait_recv(part, rbase + 2 * Z + b)
            send(part, part, sbase + 3 * Z + b, rbase + 3 * Z + b, sib)
        for b in range(Z):
            wait_recv(buf.at[rows_at(1 - tp, 1 - c, b)], rbase + 3 * Z + b)

    def gather(k, buf, wide):
        for dist in range(1, Z):
            ag_step(k, buf, dist, wide)
        ag_tail(k, buf, wide)

    CW = p.model // CHUNKS
    used = {}

    def reuse(name, k):
        before = used.get(name)
        used[name] = k
        return before

    def brecv(k):
        return brecvs.at[0 if k == 1 else 1]

    def groups(k):
        return 2 if k in (1, 2) else 1

    def bsent(k, j):
        wait_send(bsend.at[j, pl.ds(0, groups(k))], p.rb_s + k * CHUNKS + j)

    def ysent(k, j):
        wait_send(ysend.at[j], p.ry_s + k * CHUNKS + j)

    def product(terms, j, g, e):
        rows = pl.ds(pl.multiple_of((g * 2 + e) * HALF, HALF), HALF)
        cols = pl.ds(pl.multiple_of(j * CW, CW), CW)
        total = None
        for a, b in terms:
            part = dot(a[rows, :], b[cols, :], NT)
            total = part if total is None else total + part
        return total

    def own_at(j):
        return pl.ds(pl.multiple_of(j * HALF, HALF), HALF)

    def owns(k):
        return up if k == 2 else gate

    def rs_parts(k, terms):
        wide = groups(k) == 2
        mine = tp if wide else 0
        before_b = reuse("b", k)
        before_y = reuse("y", k) if wide else None

        def first(j, carry):
            values = [product(terms, j, g, 1 - c).astype(BF16) for g in range(groups(k))]
            if before_b is not None and before_b != 2:
                bsent(before_b, j)
            for g, value in enumerate(values):
                bsend[j, g] = value
            rc(
                bsend.at[j, pl.ds(0, groups(k))], brecv(k).at[j, pl.ds(0, groups(k))],
                p.rb_s + k * CHUNKS + j, p.rb_r + k * CHUNKS + j, sib,
            ).start()
            return carry

        lax.fori_loop(0, CHUNKS, first, 0)

        def second(j, carry):
            value = product(terms, j, 1 - tp, c) if wide else None
            wait_recv(brecv(k).at[j, pl.ds(0, groups(k))], p.rb_r + k * CHUNKS + j)
            owns(k)[own_at(j), :] = product(terms, j, mine, c) + brecv(k)[j, mine].astype(F32)
            if not wide:
                return carry
            if before_y is not None:
                ysent(before_y, j)
            ysend[j] = (value + brecv(k)[j, 1 - tp].astype(F32)).astype(BF16)
            rc(
                ysend.at[j], yrecv.at[k - 1, j], p.ry_s + k * CHUNKS + j, p.ry_r + k * CHUNKS + j, {"tp": 1 - tp}
            ).start()
            return carry

        lax.fori_loop(0, CHUNKS, second, 0)

    def rz_r(k, j, t):
        return p.rz_r + (k * CHUNKS + j) * (Z + 1) + t

    def zsent(k, j, t):
        wait_send(zsend.at[j, t], p.rz_s + (k * CHUNKS + j) * Z + t)

    def zslot(k):
        return zrecv.at[k % 3]

    def add_y(k, j):
        if groups(k) == 2:
            wait_recv(yrecv.at[k - 1, j], p.ry_r + k * CHUNKS + j)
            owns(k)[own_at(j), :] += yrecv[k - 1, j].astype(F32)

    def rs_ring(k, between):
        before = reuse("z", k)

        def move(j, t, near):
            upward = z < t
            has = jnp.where(upward, z > 0, z < Z - 1)
            mine = owns(k).at[pl.ds(j * HALF + t * H, H)]

            @pl.when((z != t) & (jnp.where(upward, z < Z // 2, z >= Z // 2) == near))
            def _():
                if before is not None:
                    zsent(before, j, t)

                @pl.when(has)
                def _():
                    wait_recv(zslot(k).at[j, t], rz_r(k, j, t))
                    zsend[j, t] = (mine[...] + zslot(k)[j, t].astype(F32)).astype(BF16)

                @pl.when(jnp.logical_not(has))
                def _():
                    zsend[j, t] = mine[...].astype(BF16)

                to = jnp.where(upward, up_z, down_z)
                slot = jnp.where((to == t) & jnp.logical_not(upward), Z, t)
                rc(
                    zsend.at[j, t], zslot(k).at[j, slot],
                    p.rz_s + (k * CHUNKS + j) * Z + t, rz_r(k, j, slot), {"z": to},
                ).start()

        order = (Z - 1, 0, *range(Z - 2, 0, -1))
        for j in range(CHUNKS + 1):
            if j < CHUNKS:
                add_y(k, j)
                for t in order:
                    move(j, t, True)
            if j:
                for t in order:
                    move(j - 1, t, False)
            if j < CHUNKS:
                between(j)

    def rs_finish(k):
        for j in range(CHUNKS):
            cols = slice(j * CW, (j + 1) * CW)
            acc[:, cols] = owns(k)[pl.ds(pl.multiple_of(j * HALF + z * H, H), H), :]

            @pl.when(z > 0)
            def _():
                wait_recv(zslot(k).at[j, z], rz_r(k, j, z))
                acc[:, cols] += zslot(k)[j, z].astype(F32)

            @pl.when(z < Z - 1)
            def _():
                wait_recv(zslot(k).at[j, Z], rz_r(k, j, Z))
                acc[:, cols] += zslot(k)[j, Z].astype(F32)
        return acc[...]

    def rs_direct(k, chunks):
        for j in chunks:
            bsent(k, j)
            add_y(k, j)
            bsend[j, 1] = owns(k)[own_at(j), :].astype(BF16)
            for d in range(1, Z):
                send(
                    bsend.at[j, 1, pl.ds(row_of(zplus(d), H), H)], zslot(k).at[j, d],
                    p.rz_s + (k * CHUNKS + j) * Z + d, rz_r(k, j, d), {"z": zplus(d)},
                )

    def rs_direct_finish(k):
        parts = []
        for j in range(CHUNKS):
            value = owns(k)[pl.ds(pl.multiple_of(j * HALF + z * H, H), H), :]
            for d in range(1, Z):
                wait_recv(zslot(k).at[j, d], rz_r(k, j, d))
                value = value + zslot(k)[j, d].astype(F32)
            parts.append(value)
        return jnp.concatenate(parts, axis=1)

    per = 256 // (2 * R)

    def dw_place(i, g):
        xd, zd, yd = mod(g, X), mod(lax.div(g, jnp.int32(X)), Z), lax.div(g, jnp.int32(X * Z))
        mine = (xd == x) & (yd == yh)
        return xd, zd, yd, mine if i in WIDE else mine & holder

    def dw_send(many, rows_ref, grads):
        def one(t, carry):
            cols = pl.ds(pl.multiple_of(t * 256, 256), 256)
            left = rows_ref[:, cols]
            for i, grad in zip(many, grads):
                w[i][cols, :] = dot(left, grad[...], TN).astype(BF16)
                for n in range(per):
                    g = t * per + n
                    xd, zd, yd, mine = dw_place(i, g)
                    from_me = yx_me if i in WIDE else s_me

                    @pl.when(jnp.logical_not(mine))
                    def _():
                        rc(
                            w[i].at[pl.ds(pl.multiple_of(g * 2 * R, 2 * R), 2 * R)], rb[i].at[from_me, zd],
                            p.dw_s + i * p.nseg + g, p.dw_r + (i * S + from_me) * Z + zd,
                            {"yh": yd, "x": xd, "tp": tp if i in WIDE else c},
                        ).start()
            return carry

        lax.fori_loop(0, p.model // 256, one, 0)

    def dw_sent(i):
        for g in range(p.nseg):
            mine = dw_place(i, jnp.int32(g))[3]

            @pl.when(jnp.logical_not(mine))
            def _():
                wait_send(w[i].at[pl.ds(g * 2 * R, 2 * R)], p.dw_s + i * p.nseg + g)

    def place(i, zz, cc):
        if i == 0:
            return og[0].at[zz]
        n = p.cols[i]
        return og[i].at[:, pl.ds(row_of(zz * 2 + cc if i in WIDE else zz, n), n)]

    def ogr(i, zz, cc):
        return p.og_r + (i * Z + zz) * 2 + (cc if i in WIDE else 0)

    def dw_reduce(i, zds=None):
        n = p.cols[i]
        size, me = (YX, yx_me) if i in WIDE else (S, s_me)
        items = [(zd, at, min(TMP, n - at)) for zd in (range(Z) if zds is None else zds) for at in range(0, n, TMP)]

        def tiles(q):
            zd, at, width = items[q]
            return [
                lc(
                    rb[i].at[mod(me + d, size), zd, :, pl.ds(at, width)],
                    tmp.at[q % 2, d - 1, :, pl.ds(0, width)], p.tmp_l + q % 2 * S + d,
                )
                for d in range(1, size)
            ]

        def begin(q):
            zd, at, _ = items[q]
            if at == 0:
                for d in range(1, size):
                    s = mod(me + d, size)
                    wait_recv(rb[i].at[s, zd], p.dw_r + (i * S + s) * Z + zd)
            for copy in tiles(q):
                copy.start()

        def run():
            begin(0)
            for q, (zd, at, width) in enumerate(items):
                if q + 1 < len(items):
                    begin(q + 1)
                for copy in tiles(q):
                    copy.wait()
                mine = seg(yh, zd, x)
                total = w[i][mine, at : at + width].astype(F32)
                for d in range(1, size):
                    total = total + tmp[q % 2, d - 1, :, 0:width].astype(F32)
                w[i][mine, at : at + width] = total.astype(BF16)
                if at + width < n:
                    continue
                for e in range(2):
                    src = w[i].at[block(yh, zd, x, e)]
                    here = (z == zd) & (c == e)

                    @pl.when(here)
                    def _():
                        lc(src, place(i, z, c), p.og_l + i).start()

                    @pl.when(jnp.logical_not(here))
                    def _():
                        rc(
                            src, place(i, z, c), p.og_s + (i * Z + zd) * 2 + e, ogr(i, z, c),
                            {"z": jnp.int32(zd), "core": jnp.int32(e)},
                        ).start()

        when(None if i in WIDE else holder, run)

    def dw_done(i):
        cores = range(2) if i in WIDE else (0,)
        for b in range(Z):
            for e in cores:
                here = (z == b) & ((c == e) if i in WIDE else holder)

                @pl.when(here)
                def _():
                    lc(w[i].at[block(yh, z, x, c)], place(i, z, c), p.og_l + i).wait()

                @pl.when(jnp.logical_not(here))
                def _():
                    wait_recv(place(i, jnp.int32(b), jnp.int32(e)), ogr(i, b, e))

        def sent():
            for zd in range(Z):
                for e in range(2):
                    @pl.when(jnp.logical_not((z == zd) & (c == e)))
                    def _():
                        wait_send(w[i].at[block(yh, zd, x, e)], p.og_s + (i * Z + zd) * 2 + e)

        when(None if i in WIDE else holder, sent)

    def deliver(k, out):
        dst = out.at[pl.ds(row_of(c, H), H)]
        for t in range(p.TP):
            here = holder & (tp == t)
            pl.when(here)(lambda: lc(swap.at[k], dst, p.out_l + k).start())
            send(
                swap.at[k], dst, p.out_s + k * 2 + t, p.out_r + k * 2 + c,
                {"core": tp, "tp": jnp.int32(t)}, jnp.logical_not(here),
            )

    def delivered(k, out):
        for e in range(2):
            here = holder & (c == e)

            @pl.when(here)
            def _():
                lc(swap.at[k], out.at[pl.ds(row_of(c, H), H)], p.out_l + k).wait()

            @pl.when(jnp.logical_not(here))
            def _():
                wait_recv(out.at[pl.ds(e * H, H)], p.out_r + k * 2 + e)

    def fill(point):
        for kind, *args in FILL.get(point, ()):
            if kind == "stage":
                w_stage1(args[0], args[1])
            elif kind == "forward":
                w_forward(args[0], args[1])
            elif kind == "cotangent":
                ag_step(1, gg, args[0], True)
            elif kind == "sum":
                rs_direct(2, args[0])
            else:
                dw_reduce(args[0], args[1])

    w_stage1(0)
    for n in range(2):
        wait_recv(swap.at[n], p.swap_r + n)
    mine = pl.ds(row_of(c, H), H)
    toks[...] = jnp.where(holder, tok[mine, :], swap[0])
    gg[rows_at(tp, c, z), :] = jnp.where(holder, cot[mine, :], swap[1])
    token_rows = toks[...].astype(F32)
    fill("inputs")
    factor_attn = lax.rsqrt(jnp.mean(token_rows * token_rows, axis=1, keepdims=True) + EPS)
    wait_recv(gbuf.at[pl.ds(0, p.n_ctx - 1)], p.gain_r)
    q = p.n_ctx * 128 // p.model
    gain_parts = []
    for b in range(p.model // 128):
        total = gbuf[b * q]
        for n in range(1, q):
            total = total + gbuf[b * q + n]
        gain_parts.append(total)
    gains = jnp.concatenate(gain_parts, axis=1)
    gain_attn, gain_mlp = gains[0:1, :], gains[1:2, :]
    n1[rows_at(0, c, z), :] = (token_rows * factor_attn * gain_attn).astype(BF16)
    ag_step(0, n1, 0, False)
    fill("n1_0")
    w_forward(0)
    ag_step(0, n1, 1, False)
    fill("n1_1")
    ag_step(0, n1, 2, False)
    fill("n1_2")
    ag_step(0, n1, 3, False)
    ag_tail(0, n1, False)
    fill("n1_3")
    w_wait(0)

    first_half = mod(lane, HEAD_DIM) < HEAD_DIM // 2

    def rotate(t, cosine, sine):
        turned = jnp.where(first_half, pltpu.roll(t, 96, 1), pltpu.roll(t, 32, 1))
        return t * cosine + turned * sine

    lin = dot(n1[...], w0[...], NN)
    cosine, sine = cosr[...], sinr[...]
    scale = HEAD_DIM ** (-0.5)
    pairs = p.qc // 128
    kv_lin = lin[:, p.qc : p.qc + 128]
    own_rows = pl.ds(pl.multiple_of(s_me * p.rows, p.rows), p.rows)
    kvall[own_rows, :] = jnp.where(low, rotate(kv_lin, cosine, sine), kv_lin).astype(BF16)
    for n, (a, dx, f) in enumerate(plane):
        send(kvall.at[own_rows], kvall.at[own_rows], p.kv_s + n, p.kv_r + n, away(a, 0, dx, 0, f))
    for n in range(pairs):
        turned_q = rotate(lin[:, n * 128 : (n + 1) * 128], cosine, sine).astype(BF16).astype(F32) * scale
        qpad[2 * n] = jnp.where(low, turned_q, 0.0).astype(BF16)
        qpad[2 * n + 1] = jnp.where(low, pltpu.roll(turned_q, 64, 1), 0.0).astype(BF16)

    def from_plane(a, dx, f):
        s = (mod(yh + YH - a, YH) * X + mod(x + X - dx, X)) * 2 + mod(tp + 2 - f, 2)
        return pl.ds(pl.multiple_of(s * p.rows, p.rows), p.rows)

    fill("kv")
    for n, delta in enumerate(plane):
        wait_recv(kvall.at[from_plane(*delta)], p.kv_r + n)
    fill("attend_0")
    T = p.tile
    KC = p.rows
    down = lax.broadcasted_iota(jnp.int32, (BLOCK, 1), 0)

    def masked(s, rows, scores):
        at = posq[:, rows]
        parts = []
        for b in range(2 * Z):
            allowed = down <= at - ids[s, b] * BLOCK
            parts.append(jnp.where(allowed, scores[b * BLOCK : (b + 1) * BLOCK, :], NEG))
        return jnp.concatenate(parts, axis=0)

    def keys(s):
        return pl.ds(s * KC, KC)

    for n in range(pairs):
        def attend(t, carry):
            rows = pl.ds(pl.multiple_of(t * T, T), T)
            outs = []
            for e in range(2):
                h = 2 * n + e
                query = qpad[h, rows, :]
                top = jnp.full((8, T), NEG, F32)
                for s in range(S):
                    scores = masked(s, rows, dot(kvall[keys(s), :], query, NT))
                    dkv[keys(s), :] = scores
                    top = jnp.maximum(top, jnp.max(scores.reshape(KC // 8, 8, T), axis=0))
                top = jnp.max(top, axis=0, keepdims=True)
                total = jnp.zeros((8, T), F32)
                for s in range(S):
                    grown = jnp.exp(dkv[keys(s), :] - top)
                    dkv[keys(s), :] = grown
                    total = total + jnp.sum(grown.reshape(KC // 8, 8, T), axis=0)
                total = jnp.sum(total, axis=0, keepdims=True)
                lse[h : h + 1, rows] = top + jnp.log(total)
                share = 1.0 / total
                out = jnp.zeros((128, T), F32)
                for s in range(S):
                    out = out + dot(kvall[keys(s), :], (dkv[keys(s), :] * share).astype(BF16), TN)
                outs.append(out[HEAD_DIM:, :])
            out = jnp.concatenate(outs, axis=0)
            ot[n, :, rows] = out
            mixed[rows, n * 128 : (n + 1) * 128] = jnp.transpose(out).astype(BF16)
            return carry

        lax.fori_loop(0, p.rows // T, attend, 0)
        fill(f"attend_{n + 1}")
    w_wait(1)
    rs_parts(0, [(mixed, w1)])
    rs_ring(0, lambda j: fill(f"residual_{j}"))
    residual = toks[...].astype(F32) + rs_finish(0)
    resid[...] = residual
    factor_mlp = lax.rsqrt(jnp.mean(residual * residual, axis=1, keepdims=True) + EPS)
    n2[rows_at(tp, c, z), :] = (residual * factor_mlp * gain_mlp).astype(BF16)
    ag_step(2, n2, 0, True)
    fill("n2_0")
    ag_step(2, n2, 1, True)
    fill("n2_1")
    ag_step(2, n2, 2, True)
    fill("n2_2")
    ag_step(2, n2, 3, True)
    ag_tail(2, n2, True)
    fill("n2_3")

    w_wait(2)
    w_wait(3)

    def feed(t, carry):
        cols = pl.ds(pl.multiple_of(t * 256, 256), 256)
        gate[:, cols] = dot(n2[...], w2[:, cols], NN)
        up[:, cols] = dot(n2[...], w3[:, cols], NN)
        return carry

    lax.fori_loop(0, p.fc // 256, feed, 0)
    fill("feed")
    ag_tail(1, gg, True)
    w_wait(4)

    def feed_back(t, carry):
        cols = pl.ds(pl.multiple_of(t * 256, 256), 256)
        back = dot(gg[...], w4[:, cols], NN)
        gate_pre, up_pre = gate[:, cols], up[:, cols]
        sig = jax.nn.sigmoid(gate_pre)
        silu = gate_pre * sig
        hid[:, cols] = (silu * up_pre).astype(BF16)
        dgate[:, cols] = (back * up_pre * sig * (1.0 + gate_pre * (1.0 - sig))).astype(BF16)
        dup[:, cols] = (back * silu).astype(BF16)
        return carry

    lax.fori_loop(0, p.fc // 256, feed_back, 0)
    drain = pending[:]
    pending.clear()
    for wait in drain:
        wait()
    norm_terms, out_terms = [(dgate, w2), (dup, w3)], [(hid, w4)]
    rs_parts(1, norm_terms)
    rs_parts(2, out_terms)
    for i, left, right in ((4, gg, hid), (2, n2, dgate), (3, n2, dup)):
        dw_send([i], left, [right])
    rs_ring(1, lambda j: fill(f"norm_{j}"))
    grad_norm_mlp = rs_finish(1)
    weighted = grad_norm_mlp * gain_mlp
    u = resid[...] * factor_mlp
    grad_residual = gg[rows_at(tp, c, z), :].astype(F32) + factor_mlp * (
        weighted - u * jnp.mean(weighted * u, axis=1, keepdims=True)
    )
    gain_mlp_part = jnp.sum(grad_norm_mlp * u, axis=0, keepdims=True)
    ga[rows_at(0, c, z), :] = grad_residual.astype(BF16)
    resid2[...] = grad_residual
    ag_step(3, ga, 0, False)
    fill("ga_0")
    ag_step(3, ga, 1, False)
    fill("ga_1")
    ag_step(3, ga, 2, False)
    fill("ga_2")
    ag_step(3, ga, 3, False)
    ag_tail(3, ga, False)
    fill("ga_3")

    for n in range(pairs):
        gm = dot(ga[...], w1[:, n * 128 : (n + 1) * 128], NN).astype(BF16).astype(F32)
        ot[n] = ot[n] * jnp.transpose(gm)
        gmpad[2 * n] = jnp.where(low, 0.0, pltpu.roll(gm, 64, 1)).astype(BF16)
        gmpad[2 * n + 1] = jnp.where(low, 0.0, gm).astype(BF16)
    dw_send([1], ga, [mixed])
    fill("back_0")
    dkv[:, 0:128] = jnp.zeros((p.seq, 128), F32)
    for n in range(pairs):
        def attend_back(t, carry):
            rows = pl.ds(pl.multiple_of(t * T, T), T)
            agree = ot[n, :, rows]
            outs = []
            for e in range(2):
                h = 2 * n + e
                query, back = qpad[h, rows, :], gmpad[h, rows, :]
                level = lse[h : h + 1, rows]
                delta = jnp.sum(agree[e * HEAD_DIM : (e + 1) * HEAD_DIM, :], axis=0, keepdims=True)
                out = jnp.zeros((128, T), F32)
                for s in range(S):
                    here = kvall[keys(s), :]
                    probs = jnp.exp(masked(s, rows, dot(here, query, NT)) - level)
                    ds = (probs * (dot(here, back, NT) - delta)).astype(BF16)
                    out = out + dot(here, ds, TN)
                    dkv[keys(s), 0:128] += dot(ds, query, NN) + dot(probs.astype(BF16), back, NN)
                outs.append(out[:HEAD_DIM, :])
            dq[rows, n * 128 : (n + 1) * 128] = jnp.transpose(jnp.concatenate(outs, axis=0)) * scale
            return carry

        lax.fori_loop(0, p.rows // T, attend_back, 0)
        fill(f"back_{n + 1}")
    dkv_own = dkv[own_rows, 0:128]
    for s in range(S):
        kvall[keys(s), :] = dkv[keys(s), 0:128].astype(BF16)
    for n, (a, dx, f) in enumerate(plane):
        s = (mod(yh + a, YH) * X + mod(x + dx, X)) * 2 + mod(tp + f, 2)
        send(
            kvall.at[pl.ds(pl.multiple_of(s * p.rows, p.rows), p.rows)], dkvr.at[n],
            p.dkv_s + n, p.dkv_r + n, away(a, 0, dx, 0, f),
        )
    fill("terms")
    for n in range(pairs):
        cols = slice(n * 128, (n + 1) * 128)
        gqkv[:, cols] = rotate(dq[:, cols], cosr[...], -sinr[...]).astype(BF16)
    for n in range(len(plane)):
        wait_recv(dkvr.at[n], p.dkv_r + n)
        dkv_own = dkv_own + dkvr[n].astype(F32)
    gqkv[:, p.qc : p.qc + 128] = jnp.where(low, rotate(dkv_own, cosr[...], -sinr[...]), dkv_own).astype(BF16)
    rs_parts(3, [(gqkv, w0)])
    dw_send([0], n1, [gqkv])
    rs_ring(3, lambda j: fill(f"input_{j}"))
    grad_norm_attn = rs_finish(3)
    weighted = grad_norm_attn * gain_attn
    scaled_attn = toks[...].astype(F32) * factor_attn
    swap[1] = (
        resid2[...] + factor_attn * (weighted - scaled_attn * jnp.mean(weighted * scaled_attn, axis=1, keepdims=True))
    ).astype(BF16)
    deliver(1, in_grad)

    gain_attn_part = jnp.sum(grad_norm_attn * scaled_attn, axis=0, keepdims=True)
    both_gains = jnp.concatenate([gain_attn_part, gain_mlp_part, jnp.zeros((6, p.model), F32)], axis=0)
    for b in range(p.model // 128):
        ggs[b] = both_gains[:, b * 128 : (b + 1) * 128]
    dev_me = ctx_me * p.TP + tp
    ggr[dev_me] = ggs[lax.div(ctx_me * R, jnp.int32(128))]
    for n, delta in enumerate(deltas):
        to = away(*delta)
        there = ctx_of(to["yh"], to["z"], to["x"], to["core"])
        send(ggs.at[lax.div(there * R, jnp.int32(128))], ggr.at[dev_me], p.gg_s + n, p.gg_r, to)

    fill("end_0")
    swap[0] = (resid[...] + rs_direct_finish(2)).astype(BF16)
    deliver(0, block_out)
    fill("end_1")
    wait_recv(ggr.at[pl.ds(0, p.n_dev - 1)], p.gg_r)
    total = ggr[0]
    for n in range(1, p.n_dev):
        total = total + ggr[n]
    gain_grad[...] = total

    for i in (4, 2, 3, 1, 0):
        dw_sent(i)
        dw_done(i)
    delivered(0, block_out)
    delivered(1, in_grad)
    for wait in pending:
        wait()

    def last(j, carry):
        bsent(3, j)
        ysent(2, j)
        for t in range(Z):
            pl.when(z != t)(lambda: zsent(used["z"], j, t))
        return carry

    lax.fori_loop(0, CHUNKS, last, 0)


def local(sizes, tokens, block_ids, gain_attn, w_query, key_weight, value_weight, w_out, gain_mlp,
          w_gate, w_up, w_down, cotangent):
    row_count, model = tokens.shape
    p = Plan(sizes, model, w_query.shape[1], key_weight.shape[1], w_gate.shape[1], row_count)
    YH, Z, X, S, R = p.YH, p.Z, p.X, p.S, p.R
    yh, z, x, c, tp = (lax.axis_index(a) for a in AXES)
    ctx_me = ((yh * Z + z) * X + x) * 2 + c
    s_me = (yh * X + x) * 2 + tp
    ids = block_ids.reshape(YH, Z, X, 2, 2).transpose(0, 2, 3, 4, 1).reshape(S, 2 * Z)
    positions = (ids[:, :, None] * BLOCK + jnp.arange(BLOCK, dtype=jnp.int32)).reshape(S, p.rows)
    own = lax.dynamic_slice_in_dim(positions, s_me, 1, 0)
    half = HEAD_DIM // 2
    frequencies = THETA ** (-(jnp.arange(half, dtype=F32) * 2.0 / HEAD_DIM))
    angles = own.reshape(p.rows, 1).astype(F32) * jnp.tile(frequencies, 4)[None, :]
    signs = jnp.where(jnp.arange(128) % HEAD_DIM < half, -1.0, 1.0).astype(F32)
    cosine, sine = jnp.cos(angles), jnp.sin(angles) * signs
    gains = jnp.stack([gain_attn, gain_mlp]).astype(F32)
    gin = lax.dynamic_update_slice(jnp.zeros((8, 128), F32), gains, (0, lax.rem(ctx_me * R, 128)))
    V = pl.BlockSpec(memory_space=pltpu.VMEM)
    A = pl.BlockSpec(memory_space=pl.ANY)
    H = p.half
    sd = jax.ShapeDtypeStruct
    out_shape = [sd((row_count, model), BF16), sd((row_count, model), BF16), sd((8, 128), F32)]
    out_shape += [sd((Z, R, p.cols[0]), BF16), sd(w_out.shape, BF16)] + [sd(w_gate.shape, BF16)] * 3
    out_shape += [sd((p.YX if i in WIDE else S, Z, 2 * R, n), BF16) for i, n in enumerate(p.cols)]
    CW = model // CHUNKS
    assert CW == p.fc and CHUNKS * Z * H == p.wide_rows
    scratch = [
        pltpu.VMEM((p.n_ctx, 8, 128), F32),
        pltpu.VMEM((2, H, model), BF16),
        *[pltpu.VMEM(a.shape, BF16) for a in (w_query, key_weight, value_weight)],
        pltpu.VMEM((Z, R, p.cols[0]), BF16),
        *[pltpu.VMEM((n, model), BF16) for n in (p.rows, p.wide_rows, p.wide_rows, p.rows)],
        *[pltpu.VMEM((model, n), BF16) for n in p.cols],
        pltpu.VMEM((p.qc // 64, p.rows, 128), BF16),
        pltpu.VMEM((p.qc // 64, p.rows, 128), BF16),
        pltpu.VMEM((p.seq, 128), BF16),
        pltpu.VMEM((p.seq, p.tile), F32),
        pltpu.VMEM((8, p.rows), F32),
        pltpu.VMEM((p.qc // 128, 128, p.rows), F32),
        pltpu.VMEM((p.rows, p.qc), BF16),
        *[pltpu.VMEM((p.wide_rows, p.fc), BF16) for _ in range(3)],
        *[pltpu.VMEM((p.wide_rows, p.fc), F32) for _ in range(2)],
        pltpu.VMEM((p.rows, p.qc), F32),
        pltpu.VMEM((S - 1, p.rows, 128), BF16),
        pltpu.VMEM((p.rows, p.cols[0]), BF16),
        pltpu.VMEM((CHUNKS, 2, Z * H, CW), BF16),
        pltpu.VMEM((2, CHUNKS, 2, Z * H, CW), BF16),
        pltpu.VMEM((CHUNKS, Z * H, CW), BF16),
        pltpu.VMEM((2, CHUNKS, Z * H, CW), BF16),
        pltpu.VMEM((CHUNKS, Z, H, CW), BF16),
        pltpu.VMEM((3, CHUNKS, Z + 1, H, CW), BF16),
        pltpu.VMEM((H, model), F32),
        pltpu.VMEM((H, model), BF16),
        pltpu.VMEM((H, model), F32),
        pltpu.VMEM((H, model), F32),
        pltpu.VMEM((model // 128, 8, 128), F32),
        pltpu.VMEM((p.n_dev, 8, 128), F32),
        pltpu.VMEM((2, S - 1, 2 * R, TMP), BF16),
        pltpu.SemaphoreType.DMA((p.n_send,)),
        pltpu.SemaphoreType.DMA((p.n_recv,)),
        pltpu.SemaphoreType.DMA((p.n_local,)),
    ]
    outs = pl.pallas_call(
        lambda *refs: block_kernel(p, *refs),
        out_shape=out_shape,
        in_specs=[V] * 6 + [pl.BlockSpec(memory_space=pltpu.SMEM)] + [A] * 7,
        out_specs=[A, A, V] + [A] * 10,
        scratch_shapes=scratch,
        compiler_params=pltpu.CompilerParams(
            collective_id=0, has_side_effects=True, vmem_limit_bytes=65400 * 1024
        ),
        name="block",
    )(
        tokens, cotangent, gin, cosine, sine, own, ids,
        w_query, key_weight, value_weight, w_out, w_gate, w_up, w_down,
    )
    block_out, in_grad, gain_grad = outs[:3]
    g_out, g_gate, g_up, g_down = (g.astype(F32) for g in outs[4:8])
    g_qkv = outs[3].transpose(1, 0, 2).astype(F32)
    gain_grads = lax.dynamic_slice(gain_grad, (0, lax.rem(ctx_me * R, 128)), (2, R))
    return (
        block_out,
        in_grad,
        gain_grads[0],
        g_qkv[:, :, : p.qc].reshape(R, -1),
        g_qkv[:, :, p.qc : p.qc + p.kc].reshape(R, -1),
        g_qkv[:, :, p.qc + p.kc :].reshape(R, -1),
        g_out,
        gain_grads[1],
        g_gate,
        g_up,
        g_down,
    )


def solution(mesh):
    n_ctx, tp = mesh.devices.shape
    Z = 4
    X = 2 if n_ctx == 16 else 4
    YH = n_ctx // (Z * X * 2)
    sizes = (YH, Z, X, tp)
    split = Mesh(mesh.devices.reshape(YH, Z, X, 2, tp), AXES)
    ctx = AXES[:4]
    rows, weight, vector = P(ctx, None), P(ctx, "tp"), P(ctx)
    return jax.shard_map(
        lambda *args: local(sizes, *args),
        mesh=split,
        in_specs=(rows, P(), vector, weight, weight, weight, weight, vector, weight, weight, weight, rows),
        out_specs=(rows, rows, vector, weight, weight, weight, weight, vector, weight, weight, weight),
        check_vma=False,
    )
```

```python
import math

import jax
import jax.numpy as jnp
from jax import lax
from jax.experimental import pallas as pl
from jax.experimental.pallas import tpu as pltpu
from jax.sharding import Mesh
from jax.sharding import PartitionSpec as P

HEAD_DIM = 64
BLOCK = 64
EPS = 1e-05
THETA = 500000.0
NEG = -1e30
MESH = pl.DeviceIdType.MESH
AXES = ("yh", "z", "x", "core", "tp")
NN = (((1,), (0,)), ((), ()))
NT = (((1,), (1,)), ((), ()))
TN = (((0,), (0,)), ((), ()))
F32 = jnp.float32
BF16 = jnp.bfloat16
CHUNKS = 4
WIDE = (2, 3, 4)
ALL = (0, 1, 2, 3)
FILL = {
    "inputs": [("stage", 1, ALL)],
    "n1_0": [("stage", 2, ALL)],
    "n1_3": [("cotangent", 0), ("stage", 3, ALL)],
    "kv": [("forward", 1, ALL)],
    "attend_0": [("cotangent", 1)],
    "attend_1": [("cotangent", 2), ("forward", 2, ALL), ("stage", 4, ALL)],
    "attend_2": [("cotangent", 3), ("forward", 3, ALL)],
    "n2_2": [("forward", 4, ALL)],
    "norm_0": [("grad", 4)],
    "norm_1": [("grad", 2)],
    "norm_2": [("reduce", 4, (0,)), ("grad", 3)],
    "norm_3": [("reduce", 4, (1, 2))],
    "ga_0": [("reduce", 4, (3,)), ("ring", 0)],
    "ga_1": [("ring", 1)],
    "ga_2": [("ring", 2)],
    "ga_3": [("ring", 3), ("reduce", 2, (0, 1))],
    "back_0": [("ring", 4), ("reduce", 2, (2, 3))],
    "back_1": [("reduce", 3, (0, 1))],
    "back_2": [("reduce", 3, (2, 3))],
    "terms": [("reduce", 1, ALL)],
    "end_1": [("reduce", 0, ALL)],
}


def dot(a, b, dims):
    return lax.dot_general(a, b, dims, preferred_element_type=F32)


def mod(a, n):
    return lax.rem(a, jnp.int32(n))


class Sems:
    def __init__(self):
        self.size = 0

    def take(self, count):
        first = self.size
        self.size += count
        return first


class Plan:
    def __init__(self, sizes, model, heads_cols, kv_cols, hidden_cols, tokens):
        self.YH, self.Z, self.X, self.TP = sizes
        self.n_ctx = self.YH * self.Z * self.X * 2
        self.n_dev = self.n_ctx * self.TP
        self.S = self.YH * self.X * 2
        self.YX = self.YH * self.X
        self.R = model // self.n_ctx
        self.model = model
        self.qc = heads_cols // self.Z
        self.kc = kv_cols // self.Z
        self.fc = hidden_cols // (2 * self.Z)
        self.cols = [self.qc + 2 * self.kc, self.qc, self.fc, self.fc, self.fc]
        self.half = tokens // 2
        self.rows = 2 * self.Z * self.half
        self.wide_rows = 2 * self.rows
        self.seq = self.S * self.rows
        self.nseg = self.n_ctx // 2
        self.fast = self.seq <= 2048
        self.tile = 256 if self.fast else 128
        self.tmp = 256 if self.fast else 128
        send, recv, local = Sems(), Sems(), Sems()
        W, Z, S, YX = 5, self.Z, self.S, self.YX
        self.gain_s, self.gain_r = send.take(self.n_ctx), recv.take(1)
        self.swap_s, self.swap_r = send.take(2), recv.take(2)
        self.s1_s, self.s1_r, self.s1_l = send.take(W * Z * 2), recv.take(W * Z * 2), local.take(W)
        self.s2_s, self.s2_r = send.take(W * Z * S), recv.take(W * YX * Z)
        self.ag_s, self.ag_r = send.take(4 * 5 * Z), recv.take(4 * 4 * Z)
        self.rb_s, self.rb_r = send.take(4 * CHUNKS), recv.take(4 * CHUNKS)
        self.ry_s, self.ry_r = send.take(4 * CHUNKS), recv.take(4 * CHUNKS)
        self.rz_s, self.rz_r = send.take(4 * CHUNKS * Z), recv.take(4 * CHUNKS * (Z + 1))
        self.kv_s, self.kv_r = send.take(S), recv.take(S)
        self.dkv_s, self.dkv_r = send.take(S), recv.take(S)
        self.dw_s, self.dw_r = send.take(W * self.nseg), recv.take(W * S * Z)
        self.og_s, self.og_r = send.take(W * Z * 2), recv.take(W * Z * 2)
        self.og_l = local.take(W)
        self.out_s, self.out_r, self.out_l = send.take(4), recv.take(4), local.take(2)
        self.gg_s, self.gg_r = send.take(self.n_dev), recv.take(1)
        self.tmp_l = local.take(2 * S)
        self.pack_l = local.take(3)
        self.n_send, self.n_recv, self.n_local = send.size, recv.size, local.size


def block_kernel(
    p,
    tok, cot, gin, cosr, sinr, posq, ids, wq, wk, wv, wi1, wi2, wi3, wi4,
    block_out, in_grad, gain_grad, og0, og1, og2, og3, og4, rb0, rb1, rb2, rb3, rb4,
    gbuf, swap, stq, stk, stv, pack, n1, n2, gg, ga, w0, w1, w2, w3, w4,
    qpad, gmpad, kvall, dkv, lse, ot, mixed, hid, dgate, dup, gate, up, dq, dkvr, gqkv,
    bsend, brecvs, ysend, yrecv, zsend, zrecv, acc, toks, resid, resid2, ggs, ggr, tmp,
    ssem, rsem, lsem,
):
    YH, Z, X, S, YX, R = p.YH, p.Z, p.X, p.S, p.YX, p.R
    H = p.half
    HALF = Z * H
    win = [None, wi1, wi2, wi3, wi4]
    w = [w0, w1, w2, w3, w4]
    og = [og0, og1, og2, og3, og4]
    rb = [rb0, rb1, rb2, rb3, rb4]
    yh, z, x, c, tp = (lax.axis_index(a) for a in AXES)
    sib = {"core": 1 - c}
    holder = c == tp
    other = c != tp
    ctx_of = lambda a, b, d, e: ((a * Z + b) * X + d) * 2 + e
    ctx_me = ctx_of(yh, z, x, c)
    s_me = (yh * X + x) * 2 + tp
    yx_me = yh * X + x
    zplus = lambda d: mod(z + d, Z)
    zminus = lambda d: mod(z + (Z - d), Z)
    row_of = lambda i, m: pl.multiple_of(i * m, m)
    pending = []

    def rc(src, dst, si, ri, dev):
        return pltpu.make_async_remote_copy(
            src_ref=src, dst_ref=dst, send_sem=ssem.at[si], recv_sem=rsem.at[ri],
            device_id=dev, device_id_type=MESH,
        )

    def wait_recv(dst, ri):
        rc(dst, dst, 0, ri, sib).wait_recv()

    def wait_send(src, si):
        rc(src, src, si, 0, sib).wait_send()

    def lc(src, dst, li):
        return pltpu.make_async_copy(src, dst, lsem.at[li])

    def when(pred, do):
        if pred is None:
            do()
        else:
            pl.when(pred)(do)

    def send(src, dst, si, ri, dev, pred=None):
        when(pred, lambda: rc(src, dst, si, ri, dev).start())
        pending.append(lambda: when(pred, lambda: wait_send(src, si)))

    loads = [lc(a, b, p.pack_l + n) for n, (a, b) in enumerate(((wq, stq), (wk, stk), (wv, stv)))]
    for copy in loads:
        copy.start()

    deltas = [
        (a, b, d, e, f)
        for a in range(YH) for b in range(Z) for d in range(X) for e in range(2) for f in range(p.TP)
        if a + b + d + e + f
    ]

    def away(a, b, d, e, f):
        return {
            "yh": mod(yh + a, YH), "z": mod(z + b, Z), "x": mod(x + d, X),
            "core": mod(c + e, 2), "tp": mod(tp + f, p.TP),
        }

    barrier = pltpu.get_barrier_semaphore()
    for delta in deltas:
        pl.semaphore_signal(barrier, inc=1, device_id=away(*delta), device_id_type=MESH)

    lane = lax.broadcasted_iota(jnp.int32, (1, 128), 1)
    low = lane < HEAD_DIM
    for copy in loads:
        copy.wait()
    for b in range(Z):
        pack[b, :, 0 : p.qc] = stq[:, b * p.qc : (b + 1) * p.qc]
        both = slice(b // 2 * 128, b // 2 * 128 + 128)
        key, val = stk[:, both].astype(F32), stv[:, both].astype(F32)
        if b % 2:
            pair = jnp.where(low, pltpu.roll(key, 64, 1), val)
        else:
            pair = jnp.where(low, key, pltpu.roll(val, 64, 1))
        pack[b, :, p.qc : p.qc + 128] = pair.astype(BF16)
    pl.semaphore_wait(barrier, len(deltas))

    gain_peers = [d for d in deltas if d[4] == 0]
    gbuf[ctx_me] = gin[...]
    for n, src in enumerate((tok, cot)):
        send(src.at[pl.ds(row_of(1 - c, H), H)], swap.at[n], p.swap_s + n, p.swap_r + n, sib)
    for n, delta in enumerate(gain_peers):
        send(gin, gbuf.at[ctx_me], p.gain_s + n, p.gain_r, away(*delta))

    def seg(a, b, d):
        return pl.ds(pl.multiple_of(ctx_of(a, b, d, 0) * R, 2 * R), 2 * R)

    def block(a, b, d, e):
        return pl.ds(pl.multiple_of(ctx_of(a, b, d, e) * R, R), R)

    def piece(i, zz, cc):
        if i == 0:
            return pack.at[zz]
        n = p.cols[i]
        return win[i].at[:, pl.ds(row_of(zz * 2 + cc if i in WIDE else zz, n), n)]

    def s1r(i, d, e):
        return p.s1_r + (i * Z + d) * 2 + e

    def w_stage1(i, steps=None):
        dst = w[i].at[block(yh, z, x, c)]
        for d in range(Z) if steps is None else steps:
            si = p.s1_s + (i * Z + d) * 2
            if i in WIDE:
                for e in range(2):
                    src = piece(i, zplus(d), mod(c + e, 2))
                    if d + e:
                        send(src, dst, si + e, s1r(i, d, c), {"z": zplus(d), "core": mod(c + e, 2)})
                    else:
                        lc(src, dst, p.s1_l + i).start()
                continue
            src = piece(i, zplus(d), c)
            if d == 0:
                pl.when(holder)(lambda: lc(src, dst, p.s1_l + i).start())
            send(src, dst, si, s1r(i, d, c), {"z": zplus(d), "core": tp}, other if d == 0 else None)

    plane = [(a, d, f) for a in range(YH) for d in range(X) for f in range(2) if a + d + f]
    line = [(a, d) for a in range(YH) for d in range(X) if a + d]

    def w_forward(i, steps=None):
        def arrived(d):
            zs = zminus(d)
            if d == 0:
                lc(piece(i, z, c), w[i].at[block(yh, z, x, c)], p.s1_l + i).wait()
                wait_recv(w[i].at[block(yh, z, x, 1 - c)], s1r(i, 0, 1 - c))
            else:
                for e in range(2):
                    wait_recv(w[i].at[block(yh, zs, x, e)], s1r(i, d, e))

        for d in range(Z) if steps is None else steps:
            when(None if i in WIDE else holder, lambda: arrived(d))
            part = w[i].at[seg(yh, zminus(d), x)]
            for n, peer in enumerate(line if i in WIDE else plane):
                send(
                    part, part, p.s2_s + (i * Z + d) * S + n,
                    p.s2_r + (i * YX + peer[0] * X + peer[1]) * Z + d,
                    away(peer[0], 0, peer[1], 0, 0 if i in WIDE else peer[2]),
                    None if i in WIDE else holder,
                )

    def w_wait(i):
        for a in range(YH):
            for dx in range(X):
                def wait_all():
                    for d in range(Z):
                        part = w[i].at[seg(mod(yh + YH - a, YH), zminus(d), mod(x + X - dx, X))]
                        wait_recv(part, p.s2_r + (i * YX + a * X + dx) * Z + d)
                if a + dx:
                    wait_all()
                elif i not in WIDE:
                    pl.when(other)(wait_all)

    def rows_at(g, e, b):
        return pl.ds(pl.multiple_of(((g * 2 + e) * Z + b) * H, H), H)

    up_z, down_z = jnp.minimum(z + 1, Z - 1), jnp.maximum(z - 1, 0)

    def ag_step(k, buf, dist, wide):
        g = tp if wide else 0
        rbase, sbase = p.ag_r + k * 4 * Z, p.ag_s + k * 5 * Z
        if dist == 0:
            mine = buf.at[rows_at(g, c, z)]
            send(mine, mine, sbase + z, rbase + z, {"z": up_z}, z < Z - 1)
            send(mine, mine, sbase + 4 * Z + z, rbase + z, {"z": down_z}, z > 0)
            send(mine, mine, sbase + Z + z, rbase + Z + z, sib)
            if wide:
                send(mine, mine, sbase + 2 * Z + z, rbase + 2 * Z + z, {"tp": 1 - tp})
            return
        for sign in (-1, 1):
            there = z + sign * dist
            has = (there >= 0) & (there < Z)
            b = jnp.clip(there, 0, Z - 1)
            part = buf.at[rows_at(g, c, b)]
            pl.when(has)(lambda: wait_recv(part, rbase + b))
            if dist < Z - 1:
                if sign < 0:
                    send(part, part, sbase + b, rbase + b, {"z": up_z}, has & (z < Z - 1))
                else:
                    send(part, part, sbase + b, rbase + b, {"z": down_z}, has & (z > 0))
            send(part, part, sbase + Z + b, rbase + Z + b, sib, has)
            if wide:
                send(part, part, sbase + 2 * Z + b, rbase + 2 * Z + b, {"tp": 1 - tp}, has)

    def ag_tail(k, buf, wide):
        g = tp if wide else 0
        rbase, sbase = p.ag_r + k * 4 * Z, p.ag_s + k * 5 * Z
        for b in range(Z):
            wait_recv(buf.at[rows_at(g, 1 - c, b)], rbase + Z + b)
        if not wide:
            return
        for b in range(Z):
            part = buf.at[rows_at(1 - tp, c, b)]
            wait_recv(part, rbase + 2 * Z + b)
            send(part, part, sbase + 3 * Z + b, rbase + 3 * Z + b, sib)
        for b in range(Z):
            wait_recv(buf.at[rows_at(1 - tp, 1 - c, b)], rbase + 3 * Z + b)

    def gather(k, buf, wide):
        for dist in range(1, Z):
            ag_step(k, buf, dist, wide)
        ag_tail(k, buf, wide)

    CW = p.model // CHUNKS
    used = {}

    def reuse(name, k):
        before = used.get(name)
        used[name] = k
        return before

    def brecv(k):
        return brecvs.at[0 if k == 1 else 1]

    def groups(k):
        return 2 if k in (1, 2) else 1

    def bsent(k, j):
        wait_send(bsend.at[j, pl.ds(0, groups(k))], p.rb_s + k * CHUNKS + j)

    def ysent(k, j):
        wait_send(ysend.at[j], p.ry_s + k * CHUNKS + j)

    def product(terms, j, g, e):
        rows = pl.ds(pl.multiple_of((g * 2 + e) * HALF, HALF), HALF)
        cols = pl.ds(pl.multiple_of(j * CW, CW), CW)
        total = None
        for a, b in terms:
            part = dot(a[rows, :], b[cols, :], NT)
            total = part if total is None else total + part
        return total

    def own_at(j):
        return pl.ds(pl.multiple_of(j * HALF, HALF), HALF)

    def owns(k):
        return up if k == 2 else gate

    def rs_parts(k, terms):
        wide = groups(k) == 2
        mine = tp if wide else 0
        before_b = reuse("b", k)
        before_y = reuse("y", k) if wide else None

        def first(j, carry):
            values = [product(terms, j, g, 1 - c).astype(BF16) for g in range(groups(k))]
            if before_b is not None:
                bsent(before_b, j)
            for g, value in enumerate(values):
                bsend[j, g] = value
            rc(
                bsend.at[j, pl.ds(0, groups(k))], brecv(k).at[j, pl.ds(0, groups(k))],
                p.rb_s + k * CHUNKS + j, p.rb_r + k * CHUNKS + j, sib,
            ).start()
            return carry

        lax.fori_loop(0, CHUNKS, first, 0)

        def second(j, carry):
            value = product(terms, j, 1 - tp, c) if wide else None
            wait_recv(brecv(k).at[j, pl.ds(0, groups(k))], p.rb_r + k * CHUNKS + j)
            owns(k)[own_at(j), :] = product(terms, j, mine, c) + brecv(k)[j, mine].astype(F32)
            if not wide:
                return carry
            if before_y is not None:
                ysent(before_y, j)
            ysend[j] = (value + brecv(k)[j, 1 - tp].astype(F32)).astype(BF16)
            rc(
                ysend.at[j], yrecv.at[k - 1, j], p.ry_s + k * CHUNKS + j, p.ry_r + k * CHUNKS + j, {"tp": 1 - tp}
            ).start()
            return carry

        lax.fori_loop(0, CHUNKS, second, 0)

    def rz_r(k, j, t):
        return p.rz_r + (k * CHUNKS + j) * (Z + 1) + t

    def zsent(k, j, t):
        wait_send(zsend.at[j, t], p.rz_s + (k * CHUNKS + j) * Z + t)

    def zslot(k):
        return zrecv.at[k % 3]

    def add_y(k, j):
        if groups(k) == 2:
            wait_recv(yrecv.at[k - 1, j], p.ry_r + k * CHUNKS + j)
            owns(k)[own_at(j), :] += yrecv[k - 1, j].astype(F32)

    rings = {}

    def ring_step(k, step):
        if step == 0:
            rings[k] = reuse("z", k)
        before = rings[k]

        def move(j, t, near):
            upward = z < t
            has = jnp.where(upward, z > 0, z < Z - 1)
            mine = owns(k).at[pl.ds(j * HALF + t * H, H)]

            @pl.when((z != t) & (jnp.where(upward, z < Z // 2, z >= Z // 2) == near))
            def _():
                if before is not None:
                    zsent(before, j, t)

                @pl.when(has)
                def _():
                    wait_recv(zslot(k).at[j, t], rz_r(k, j, t))
                    zsend[j, t] = (mine[...] + zslot(k)[j, t].astype(F32)).astype(BF16)

                @pl.when(jnp.logical_not(has))
                def _():
                    zsend[j, t] = mine[...].astype(BF16)

                to = jnp.where(upward, up_z, down_z)
                slot = jnp.where((to == t) & jnp.logical_not(upward), Z, t)
                rc(
                    zsend.at[j, t], zslot(k).at[j, slot],
                    p.rz_s + (k * CHUNKS + j) * Z + t, rz_r(k, j, slot), {"z": to},
                ).start()

        order = (Z - 1, 0, *range(Z - 2, 0, -1))
        if step < CHUNKS:
            add_y(k, step)
            for t in order:
                move(step, t, True)
        if step:
            for t in order:
                move(step - 1, t, False)

    def rs_ring(k, between):
        for step in range(CHUNKS + 1):
            ring_step(k, step)
            if step < CHUNKS:
                between(step)

    def rs_finish(k):
        for j in range(CHUNKS):
            cols = slice(j * CW, (j + 1) * CW)
            acc[:, cols] = owns(k)[pl.ds(pl.multiple_of(j * HALF + z * H, H), H), :]

            @pl.when(z > 0)
            def _():
                wait_recv(zslot(k).at[j, z], rz_r(k, j, z))
                acc[:, cols] += zslot(k)[j, z].astype(F32)

            @pl.when(z < Z - 1)
            def _():
                wait_recv(zslot(k).at[j, Z], rz_r(k, j, Z))
                acc[:, cols] += zslot(k)[j, Z].astype(F32)
        return acc[...]

    per = 256 // (2 * R)

    def dw_place(i, g):
        xd, zd, yd = mod(g, X), mod(lax.div(g, jnp.int32(X)), Z), lax.div(g, jnp.int32(X * Z))
        mine = (xd == x) & (yd == yh)
        return xd, zd, yd, mine if i in WIDE else mine & holder

    def dw_send(i, rows_ref, grad):
        def one(t, carry):
            cols = pl.ds(pl.multiple_of(t * 256, 256), 256)
            w[i][cols, :] = dot(rows_ref[:, cols], grad[...], TN).astype(BF16)
            for n in range(per):
                g = t * per + n
                xd, zd, yd, mine = dw_place(i, g)
                from_me = yx_me if i in WIDE else s_me

                @pl.when(jnp.logical_not(mine))
                def _():
                    rc(
                        w[i].at[pl.ds(pl.multiple_of(g * 2 * R, 2 * R), 2 * R)], rb[i].at[from_me, zd],
                        p.dw_s + i * p.nseg + g, p.dw_r + (i * S + from_me) * Z + zd,
                        {"yh": yd, "x": xd, "tp": tp if i in WIDE else c},
                    ).start()
            return carry

        lax.fori_loop(0, p.model // 256, one, 0)

    def dw_sent(i):
        for g in range(p.nseg):
            mine = dw_place(i, jnp.int32(g))[3]

            @pl.when(jnp.logical_not(mine))
            def _():
                wait_send(w[i].at[pl.ds(g * 2 * R, 2 * R)], p.dw_s + i * p.nseg + g)

    def place(i, zz, cc):
        if i == 0:
            return og[0].at[zz]
        n = p.cols[i]
        return og[i].at[:, pl.ds(row_of(zz * 2 + cc if i in WIDE else zz, n), n)]

    def ogr(i, zz, cc):
        return p.og_r + (i * Z + zz) * 2 + (cc if i in WIDE else 0)

    def dw_reduce(i, zds=None):
        n = p.cols[i]
        size, me = (YX, yx_me) if i in WIDE else (S, s_me)
        items = [(zd, at, min(p.tmp, n - at)) for zd in (range(Z) if zds is None else zds) for at in range(0, n, p.tmp)]

        def tiles(q):
            zd, at, width = items[q]
            return [
                lc(
                    rb[i].at[mod(me + d, size), zd, :, pl.ds(at, width)],
                    tmp.at[q % 2, d - 1, :, pl.ds(0, width)], p.tmp_l + q % 2 * S + d,
                )
                for d in range(1, size)
            ]

        def begin(q):
            zd, at, _ = items[q]
            if at == 0:
                for d in range(1, size):
                    s = mod(me + d, size)
                    wait_recv(rb[i].at[s, zd], p.dw_r + (i * S + s) * Z + zd)
            for copy in tiles(q):
                copy.start()

        def run():
            begin(0)
            for q, (zd, at, width) in enumerate(items):
                if q + 1 < len(items):
                    begin(q + 1)
                for copy in tiles(q):
                    copy.wait()
                mine = seg(yh, zd, x)
                total = w[i][mine, at : at + width].astype(F32)
                for d in range(1, size):
                    total = total + tmp[q % 2, d - 1, :, 0:width].astype(F32)
                w[i][mine, at : at + width] = total.astype(BF16)
                if at + width < n:
                    continue
                for e in range(2):
                    src = w[i].at[block(yh, zd, x, e)]
                    here = (z == zd) & (c == e)

                    @pl.when(here)
                    def _():
                        lc(src, place(i, z, c), p.og_l + i).start()

                    @pl.when(jnp.logical_not(here))
                    def _():
                        rc(
                            src, place(i, z, c), p.og_s + (i * Z + zd) * 2 + e, ogr(i, z, c),
                            {"z": jnp.int32(zd), "core": jnp.int32(e)},
                        ).start()

        when(None if i in WIDE else holder, run)

    def dw_done(i):
        cores = range(2) if i in WIDE else (0,)
        for b in range(Z):
            for e in cores:
                here = (z == b) & ((c == e) if i in WIDE else holder)

                @pl.when(here)
                def _():
                    lc(w[i].at[block(yh, z, x, c)], place(i, z, c), p.og_l + i).wait()

                @pl.when(jnp.logical_not(here))
                def _():
                    wait_recv(place(i, jnp.int32(b), jnp.int32(e)), ogr(i, b, e))

        def sent():
            for zd in range(Z):
                for e in range(2):
                    @pl.when(jnp.logical_not((z == zd) & (c == e)))
                    def _():
                        wait_send(w[i].at[block(yh, zd, x, e)], p.og_s + (i * Z + zd) * 2 + e)

        when(None if i in WIDE else holder, sent)

    def deliver(k, out):
        dst = out.at[pl.ds(row_of(c, H), H)]
        for t in range(p.TP):
            here = holder & (tp == t)
            pl.when(here)(lambda: lc(swap.at[k], dst, p.out_l + k).start())
            send(
                swap.at[k], dst, p.out_s + k * 2 + t, p.out_r + k * 2 + c,
                {"core": tp, "tp": jnp.int32(t)}, jnp.logical_not(here),
            )

    def delivered(k, out):
        for e in range(2):
            here = holder & (c == e)

            @pl.when(here)
            def _():
                lc(swap.at[k], out.at[pl.ds(row_of(c, H), H)], p.out_l + k).wait()

            @pl.when(jnp.logical_not(here))
            def _():
                wait_recv(out.at[pl.ds(e * H, H)], p.out_r + k * 2 + e)

    def fill(point):
        for kind, *args in FILL.get(point, ()):
            if kind == "stage":
                w_stage1(args[0], args[1])
            elif kind == "forward":
                w_forward(args[0], args[1])
            elif kind == "cotangent":
                ag_step(1, gg, args[0], True)
            elif kind == "ring":
                ring_step(2, args[0])
            elif kind == "grad":
                dw_send(args[0], gg if args[0] == 4 else n2, {4: hid, 2: dgate, 3: dup}[args[0]])
            else:
                dw_reduce(args[0], args[1])

    w_stage1(0)
    for n in range(2):
        wait_recv(swap.at[n], p.swap_r + n)
    mine = pl.ds(row_of(c, H), H)
    toks[...] = jnp.where(holder, tok[mine, :], swap[0])
    gg[rows_at(tp, c, z), :] = jnp.where(holder, cot[mine, :], swap[1])
    token_rows = toks[...].astype(F32)
    fill("inputs")
    factor_attn = lax.rsqrt(jnp.mean(token_rows * token_rows, axis=1, keepdims=True) + EPS)
    wait_recv(gbuf.at[pl.ds(0, p.n_ctx - 1)], p.gain_r)
    q = p.n_ctx * 128 // p.model
    gain_parts = []
    for b in range(p.model // 128):
        total = gbuf[b * q]
        for n in range(1, q):
            total = total + gbuf[b * q + n]
        gain_parts.append(total)
    gains = jnp.concatenate(gain_parts, axis=1)
    gain_attn, gain_mlp = gains[0:1, :], gains[1:2, :]
    n1[rows_at(0, c, z), :] = (token_rows * factor_attn * gain_attn).astype(BF16)
    ag_step(0, n1, 0, False)
    fill("n1_0")
    w_forward(0)
    ag_step(0, n1, 1, False)
    fill("n1_1")
    ag_step(0, n1, 2, False)
    fill("n1_2")
    ag_step(0, n1, 3, False)
    ag_tail(0, n1, False)
    fill("n1_3")
    w_wait(0)

    first_half = mod(lane, HEAD_DIM) < HEAD_DIM // 2

    def rotate(t, cosine, sine):
        turned = jnp.where(first_half, pltpu.roll(t, 96, 1), pltpu.roll(t, 32, 1))
        return t * cosine + turned * sine

    lin = dot(n1[...], w0[...], NN)
    cosine, sine = cosr[...], sinr[...]
    scale = HEAD_DIM ** (-0.5)
    pairs = p.qc // 128
    kv_lin = lin[:, p.qc : p.qc + 128]
    own_rows = pl.ds(pl.multiple_of(s_me * p.rows, p.rows), p.rows)
    kvall[own_rows, :] = jnp.where(low, rotate(kv_lin, cosine, sine), kv_lin).astype(BF16)
    for n, (a, dx, f) in enumerate(plane):
        send(kvall.at[own_rows], kvall.at[own_rows], p.kv_s + n, p.kv_r + n, away(a, 0, dx, 0, f))
    for n in range(pairs):
        turned_q = rotate(lin[:, n * 128 : (n + 1) * 128], cosine, sine).astype(BF16).astype(F32) * scale
        qpad[2 * n] = jnp.where(low, turned_q, 0.0).astype(BF16)
        qpad[2 * n + 1] = jnp.where(low, pltpu.roll(turned_q, 64, 1), 0.0).astype(BF16)

    def from_plane(a, dx, f):
        s = (mod(yh + YH - a, YH) * X + mod(x + X - dx, X)) * 2 + mod(tp + 2 - f, 2)
        return pl.ds(pl.multiple_of(s * p.rows, p.rows), p.rows)

    fill("kv")
    for n, delta in enumerate(plane):
        wait_recv(kvall.at[from_plane(*delta)], p.kv_r + n)
    fill("attend_0")
    T = p.tile
    KC = p.rows
    down = lax.broadcasted_iota(jnp.int32, (BLOCK, 1), 0)

    def masked(s, rows, scores):
        at = posq[:, rows]
        parts = []
        for b in range(2 * Z):
            allowed = down <= at - ids[s, b] * BLOCK
            parts.append(jnp.where(allowed, scores[b * BLOCK : (b + 1) * BLOCK, :], NEG))
        return jnp.concatenate(parts, axis=0)

    def keys(s):
        return pl.ds(s * KC, KC)

    for n in range(pairs):
        def attend(t, carry):
            rows = pl.ds(pl.multiple_of(t * T, T), T)
            outs = []
            for e in range(2):
                h = 2 * n + e
                query = qpad[h, rows, :]
                top = jnp.full((8, T), NEG, F32)
                for s in range(S):
                    scores = masked(s, rows, dot(kvall[keys(s), :], query, NT))
                    dkv[keys(s), :] = scores
                    top = jnp.maximum(top, jnp.max(scores.reshape(KC // 8, 8, T), axis=0))
                top = jnp.max(top, axis=0, keepdims=True)
                total = jnp.zeros((8, T), F32)
                for s in range(S):
                    grown = jnp.exp(dkv[keys(s), :] - top)
                    dkv[keys(s), :] = grown
                    total = total + jnp.sum(grown.reshape(KC // 8, 8, T), axis=0)
                total = jnp.sum(total, axis=0, keepdims=True)
                lse[h : h + 1, rows] = top + jnp.log(total)
                share = 1.0 / total
                out = jnp.zeros((128, T), F32)
                for s in range(S):
                    out = out + dot(kvall[keys(s), :], (dkv[keys(s), :] * share).astype(BF16), TN)
                outs.append(out[HEAD_DIM:, :])
            out = jnp.concatenate(outs, axis=0)
            ot[n, :, rows] = out
            mixed[rows, n * 128 : (n + 1) * 128] = jnp.transpose(out).astype(BF16)
            return carry

        lax.fori_loop(0, p.rows // T, attend, 0)
        fill(f"attend_{n + 1}")
    w_wait(1)
    rs_parts(0, [(mixed, w1)])
    rs_ring(0, lambda j: fill(f"residual_{j}"))
    residual = toks[...].astype(F32) + rs_finish(0)
    resid[...] = residual
    factor_mlp = lax.rsqrt(jnp.mean(residual * residual, axis=1, keepdims=True) + EPS)
    n2[rows_at(tp, c, z), :] = (residual * factor_mlp * gain_mlp).astype(BF16)
    ag_step(2, n2, 0, True)
    fill("n2_0")
    ag_step(2, n2, 1, True)
    fill("n2_1")
    ag_step(2, n2, 2, True)
    fill("n2_2")
    ag_step(2, n2, 3, True)
    ag_tail(2, n2, True)
    fill("n2_3")

    w_wait(2)
    w_wait(3)

    def feed(t, carry):
        cols = pl.ds(pl.multiple_of(t * 256, 256), 256)
        gate[:, cols] = dot(n2[...], w2[:, cols], NN)
        up[:, cols] = dot(n2[...], w3[:, cols], NN)
        return carry

    lax.fori_loop(0, p.fc // 256, feed, 0)
    fill("feed")
    ag_tail(1, gg, True)
    w_wait(4)

    def feed_back(t, carry):
        cols = pl.ds(pl.multiple_of(t * 256, 256), 256)
        back = dot(gg[...], w4[:, cols], NN)
        gate_pre, up_pre = gate[:, cols], up[:, cols]
        sig = jax.nn.sigmoid(gate_pre)
        silu = gate_pre * sig
        hid[:, cols] = (silu * up_pre).astype(BF16)
        dgate[:, cols] = (back * up_pre * sig * (1.0 + gate_pre * (1.0 - sig))).astype(BF16)
        dup[:, cols] = (back * silu).astype(BF16)
        return carry

    lax.fori_loop(0, p.fc // 256, feed_back, 0)
    drain = pending[:]
    pending.clear()
    for wait in drain:
        wait()
    norm_terms, out_terms = [(dgate, w2), (dup, w3)], [(hid, w4)]
    rs_parts(1, norm_terms)
    rs_parts(2, out_terms)
    rs_ring(1, lambda j: fill(f"norm_{j}"))
    grad_norm_mlp = rs_finish(1)
    weighted = grad_norm_mlp * gain_mlp
    u = resid[...] * factor_mlp
    grad_residual = gg[rows_at(tp, c, z), :].astype(F32) + factor_mlp * (
        weighted - u * jnp.mean(weighted * u, axis=1, keepdims=True)
    )
    gain_mlp_part = jnp.sum(grad_norm_mlp * u, axis=0, keepdims=True)
    ga[rows_at(0, c, z), :] = grad_residual.astype(BF16)
    resid2[...] = grad_residual
    ag_step(3, ga, 0, False)
    fill("ga_0")
    ag_step(3, ga, 1, False)
    fill("ga_1")
    ag_step(3, ga, 2, False)
    fill("ga_2")
    ag_step(3, ga, 3, False)
    ag_tail(3, ga, False)
    fill("ga_3")

    for n in range(pairs):
        gm = dot(ga[...], w1[:, n * 128 : (n + 1) * 128], NN).astype(BF16).astype(F32)
        ot[n] = ot[n] * jnp.transpose(gm)
        gmpad[2 * n] = jnp.where(low, 0.0, pltpu.roll(gm, 64, 1)).astype(BF16)
        gmpad[2 * n + 1] = jnp.where(low, 0.0, gm).astype(BF16)
    dw_send(1, ga, mixed)
    fill("back_0")
    dkv[:, 0:128] = jnp.zeros((p.seq, 128), F32)
    for n in range(pairs):
        def attend_back(t, carry):
            rows = pl.ds(pl.multiple_of(t * T, T), T)
            agree = ot[n, :, rows]
            outs = []
            for e in range(2):
                h = 2 * n + e
                query, back = qpad[h, rows, :], gmpad[h, rows, :]
                level = lse[h : h + 1, rows]
                delta = jnp.sum(agree[e * HEAD_DIM : (e + 1) * HEAD_DIM, :], axis=0, keepdims=True)
                out = jnp.zeros((128, T), F32)
                for s in range(S):
                    here = kvall[keys(s), :]
                    probs = jnp.exp(masked(s, rows, dot(here, query, NT)) - level)
                    ds = (probs * (dot(here, back, NT) - delta)).astype(BF16)
                    out = out + dot(here, ds, TN)
                    dkv[keys(s), 0:128] += dot(ds, query, NN) + dot(probs.astype(BF16), back, NN)
                outs.append(out[:HEAD_DIM, :])
            dq[rows, n * 128 : (n + 1) * 128] = jnp.transpose(jnp.concatenate(outs, axis=0)) * scale
            return carry

        lax.fori_loop(0, p.rows // T, attend_back, 0)
        fill(f"back_{n + 1}")
    dkv_own = dkv[own_rows, 0:128]
    for s in range(S):
        kvall[keys(s), :] = dkv[keys(s), 0:128].astype(BF16)
    for n, (a, dx, f) in enumerate(plane):
        s = (mod(yh + a, YH) * X + mod(x + dx, X)) * 2 + mod(tp + f, 2)
        send(
            kvall.at[pl.ds(pl.multiple_of(s * p.rows, p.rows), p.rows)], dkvr.at[n],
            p.dkv_s + n, p.dkv_r + n, away(a, 0, dx, 0, f),
        )
    fill("terms")
    for n in range(pairs):
        cols = slice(n * 128, (n + 1) * 128)
        gqkv[:, cols] = rotate(dq[:, cols], cosr[...], -sinr[...]).astype(BF16)
    for n in range(len(plane)):
        wait_recv(dkvr.at[n], p.dkv_r + n)
        dkv_own = dkv_own + dkvr[n].astype(F32)
    gqkv[:, p.qc : p.qc + 128] = jnp.where(low, rotate(dkv_own, cosr[...], -sinr[...]), dkv_own).astype(BF16)
    rs_parts(3, [(gqkv, w0)])
    dw_send(0, n1, gqkv)
    rs_ring(3, lambda j: fill(f"input_{j}"))
    grad_norm_attn = rs_finish(3)
    weighted = grad_norm_attn * gain_attn
    scaled_attn = toks[...].astype(F32) * factor_attn
    swap[1] = (
        resid2[...] + factor_attn * (weighted - scaled_attn * jnp.mean(weighted * scaled_attn, axis=1, keepdims=True))
    ).astype(BF16)
    deliver(1, in_grad)

    gain_attn_part = jnp.sum(grad_norm_attn * scaled_attn, axis=0, keepdims=True)
    both_gains = jnp.concatenate([gain_attn_part, gain_mlp_part, jnp.zeros((6, p.model), F32)], axis=0)
    for b in range(p.model // 128):
        ggs[b] = both_gains[:, b * 128 : (b + 1) * 128]
    dev_me = ctx_me * p.TP + tp
    ggr[dev_me] = ggs[lax.div(ctx_me * R, jnp.int32(128))]
    for n, delta in enumerate(deltas):
        to = away(*delta)
        there = ctx_of(to["yh"], to["z"], to["x"], to["core"])
        send(ggs.at[lax.div(there * R, jnp.int32(128))], ggr.at[dev_me], p.gg_s + n, p.gg_r, to)

    fill("end_0")
    swap[0] = (resid[...] + rs_finish(2)).astype(BF16)
    deliver(0, block_out)
    fill("end_1")
    wait_recv(ggr.at[pl.ds(0, p.n_dev - 1)], p.gg_r)
    total = ggr[0]
    for n in range(1, p.n_dev):
        total = total + ggr[n]
    gain_grad[...] = total

    for i in (4, 2, 3, 1, 0):
        dw_sent(i)
        dw_done(i)
    delivered(0, block_out)
    delivered(1, in_grad)
    for wait in pending:
        wait()

    def last(j, carry):
        bsent(3, j)
        ysent(2, j)
        for t in range(Z):
            pl.when(z != t)(lambda: zsent(used["z"], j, t))
        return carry

    lax.fori_loop(0, CHUNKS, last, 0)


def unpack_kernel(
    p, g0, g1, g2, g3, g4, rows0, rows1, o_q, o_k, o_v, o1, o2, o3, o4, out0, out1,
    s0, s1, s2, s3, s4, s5, s6, t_q, t_k, t_v, t1, t2, t3, t4, sem,
):
    copies = []
    pairs = [(g0, s0), (g2, s2), (g3, s3), (g4, s4), (g1, s1), (rows0, s5), (rows1, s6)]
    loads = [pltpu.make_async_copy(a, b, sem.at[n]) for n, (a, b) in enumerate(pairs)]
    for copy in loads:
        copy.start()

    def store(src, dst, n):
        copy = pltpu.make_async_copy(src, dst, sem.at[7 + n])
        copy.start()
        copies.append(copy)

    loads[0].wait()
    low = lax.broadcasted_iota(jnp.int32, (1, 128), 1) < HEAD_DIM
    for b in range(p.Z):
        t_q[:, b * p.qc : (b + 1) * p.qc] = s0[b, :, 0 : p.qc].astype(F32)
    for b in range(0, p.Z, 2):
        one, two = (s0[b + n, :, p.qc : p.qc + 128].astype(F32) for n in range(2))
        both = slice(b * HEAD_DIM, b * HEAD_DIM + 128)
        t_k[:, both] = jnp.where(low, one, pltpu.roll(two, 64, 1))
        t_v[:, both] = jnp.where(low, pltpu.roll(one, 64, 1), two)
    for n, (t, o) in enumerate(((t_q, o_q), (t_k, o_k), (t_v, o_v))):
        store(t, o, n)
    for n, (src, t, o) in enumerate(((s2, t2, o2), (s3, t3, o3), (s4, t4, o4), (s1, t1, o1))):
        loads[n + 1].wait()
        t[...] = src[...].astype(F32)
        store(t, o, n + 3)
    for n, (src, o) in enumerate(((s5, out0), (s6, out1))):
        loads[n + 5].wait()
        store(src, o, n + 7)
    for copy in copies:
        copy.wait()


def local(sizes, tokens, block_ids, gain_attn, w_query, key_weight, value_weight, w_out, gain_mlp,
          w_gate, w_up, w_down, cotangent):
    row_count, model = tokens.shape
    p = Plan(sizes, model, w_query.shape[1], key_weight.shape[1], w_gate.shape[1], row_count)
    YH, Z, X, S, R = p.YH, p.Z, p.X, p.S, p.R
    yh, z, x, c, tp = (lax.axis_index(a) for a in AXES)
    ctx_me = ((yh * Z + z) * X + x) * 2 + c
    s_me = (yh * X + x) * 2 + tp
    ids = block_ids.reshape(YH, Z, X, 2, 2).transpose(0, 2, 3, 4, 1).reshape(S, 2 * Z)
    positions = (ids[:, :, None] * BLOCK + jnp.arange(BLOCK, dtype=jnp.int32)).reshape(S, p.rows)
    own = lax.dynamic_slice_in_dim(positions, s_me, 1, 0)
    half = HEAD_DIM // 2
    frequencies = THETA ** (-(jnp.arange(half, dtype=F32) * 2.0 / HEAD_DIM))
    angles = own.reshape(p.rows, 1).astype(F32) * jnp.tile(frequencies, 4)[None, :]
    signs = jnp.where(jnp.arange(128) % HEAD_DIM < half, -1.0, 1.0).astype(F32)
    cosine, sine = jnp.cos(angles), jnp.sin(angles) * signs
    gains = jnp.stack([gain_attn, gain_mlp]).astype(F32)
    gin = lax.dynamic_update_slice(jnp.zeros((8, 128), F32), gains, (0, lax.rem(ctx_me * R, 128)))
    V = pl.BlockSpec(memory_space=pltpu.VMEM)
    A = pl.BlockSpec(memory_space=pl.ANY)
    H = p.half
    sd = jax.ShapeDtypeStruct
    out_shape = [sd((row_count, model), BF16), sd((row_count, model), BF16), sd((8, 128), F32)]
    out_shape += [sd((Z, R, p.cols[0]), BF16), sd(w_out.shape, BF16)] + [sd(w_gate.shape, BF16)] * 3
    out_shape += [sd((p.YX if i in WIDE else S, Z, 2 * R, n), BF16) for i, n in enumerate(p.cols)]
    CW = model // CHUNKS
    assert CW == p.fc and CHUNKS * Z * H == p.wide_rows
    scratch = [
        pltpu.VMEM((p.n_ctx, 8, 128), F32),
        pltpu.VMEM((2, H, model), BF16),
        *[pltpu.VMEM(a.shape, BF16) for a in (w_query, key_weight, value_weight)],
        pltpu.VMEM((Z, R, p.cols[0]), BF16),
        *[pltpu.VMEM((n, model), BF16) for n in (p.rows, p.wide_rows, p.wide_rows, p.rows)],
        *[pltpu.VMEM((model, n), BF16) for n in p.cols],
        pltpu.VMEM((p.qc // 64, p.rows, 128), BF16),
        pltpu.VMEM((p.qc // 64, p.rows, 128), BF16),
        pltpu.VMEM((p.seq, 128), BF16),
        pltpu.VMEM((p.seq, p.tile), F32),
        pltpu.VMEM((8, p.rows), F32),
        pltpu.VMEM((p.qc // 128, 128, p.rows), F32),
        pltpu.VMEM((p.rows, p.qc), BF16),
        *[pltpu.VMEM((p.wide_rows, p.fc), BF16) for _ in range(3)],
        *[pltpu.VMEM((p.wide_rows, p.fc), F32) for _ in range(2)],
        pltpu.VMEM((p.rows, p.qc), F32),
        pltpu.VMEM((S - 1, p.rows, 128), BF16),
        pltpu.VMEM((p.rows, p.cols[0]), BF16),
        pltpu.VMEM((CHUNKS, 2, Z * H, CW), BF16),
        pltpu.VMEM((2, CHUNKS, 2, Z * H, CW), BF16),
        pltpu.VMEM((CHUNKS, Z * H, CW), BF16),
        pltpu.VMEM((2, CHUNKS, Z * H, CW), BF16),
        pltpu.VMEM((CHUNKS, Z, H, CW), BF16),
        pltpu.VMEM((3, CHUNKS, Z + 1, H, CW), BF16),
        pltpu.VMEM((H, model), F32),
        pltpu.VMEM((H, model), BF16),
        pltpu.VMEM((H, model), F32),
        pltpu.VMEM((H, model), F32),
        pltpu.VMEM((model // 128, 8, 128), F32),
        pltpu.VMEM((p.n_dev, 8, 128), F32),
        pltpu.VMEM((2, S - 1, 2 * R, p.tmp), BF16),
        pltpu.SemaphoreType.DMA((p.n_send,)),
        pltpu.SemaphoreType.DMA((p.n_recv,)),
        pltpu.SemaphoreType.DMA((p.n_local,)),
    ]
    outs = pl.pallas_call(
        lambda *refs: block_kernel(p, *refs),
        out_shape=out_shape,
        in_specs=[V] * 6 + [pl.BlockSpec(memory_space=pltpu.SMEM)] + [A] * 7,
        out_specs=[A, A, V] + [A] * 10,
        scratch_shapes=scratch,
        compiler_params=pltpu.CompilerParams(
            collective_id=0, has_side_effects=True, vmem_limit_bytes=65400 * 1024
        ),
        name="block",
    )(
        tokens, cotangent, gin, cosine, sine, own, ids,
        w_query, key_weight, value_weight, w_out, w_gate, w_up, w_down,
    )
    gain_grad, grads = outs[2], list(outs[3:8])
    shapes = [a.shape for a in (w_query, key_weight, value_weight, w_out, w_gate, w_up, w_down)]
    unpacked = pl.pallas_call(
        lambda *refs: unpack_kernel(p, *refs),
        out_shape=[sd(a, F32) for a in shapes] + [sd((row_count, model), BF16)] * 2,
        in_specs=[A] * 7,
        out_specs=[A] * 9,
        scratch_shapes=[
            *[pltpu.VMEM(g.shape, BF16) for g in grads + list(outs[:2])],
            *[pltpu.VMEM(a, F32) for a in shapes],
            pltpu.SemaphoreType.DMA((16,)),
        ],
        compiler_params=pltpu.CompilerParams(vmem_limit_bytes=65400 * 1024),
        name="unpack",
    )(*grads, outs[0], outs[1])
    g_query, g_key, g_value, g_out, g_gate, g_up, g_down, block_out, in_grad = unpacked
    gain_grads = lax.dynamic_slice(gain_grad, (0, lax.rem(ctx_me * R, 128)), (2, R))
    return (
        block_out, in_grad, gain_grads[0], g_query, g_key, g_value, g_out, gain_grads[1], g_gate, g_up, g_down,
    )


def solution(mesh):
    n_ctx, tp = mesh.devices.shape
    Z = 4
    X = 2 if n_ctx == 16 else 4
    YH = n_ctx // (Z * X * 2)
    sizes = (YH, Z, X, tp)
    split = Mesh(mesh.devices.reshape(YH, Z, X, 2, tp), AXES)
    ctx = AXES[:4]
    rows, weight, vector = P(ctx, None), P(ctx, "tp"), P(ctx)
    return jax.shard_map(
        lambda *args: local(sizes, *args),
        mesh=split,
        in_specs=(rows, P(), vector, weight, weight, weight, weight, vector, weight, weight, weight, rows),
        out_specs=(rows, rows, vector, weight, weight, weight, weight, vector, weight, weight, weight),
        check_vma=False,
    )
```

```python
import math

import jax
import jax.numpy as jnp
from jax import lax
from jax.experimental import pallas as pl
from jax.experimental.pallas import tpu as pltpu
from jax.sharding import Mesh
from jax.sharding import PartitionSpec as P

HEAD_DIM = 64
BLOCK = 64
EPS = 1e-05
THETA = 500000.0
NEG = -1e30
MESH = pl.DeviceIdType.MESH
AXES = ("yh", "z", "x", "core", "tp")
NN = (((1,), (0,)), ((), ()))
NT = (((1,), (1,)), ((), ()))
TN = (((0,), (0,)), ((), ()))
F32 = jnp.float32
BF16 = jnp.bfloat16
CHUNKS = 4
WIDE = (2, 3, 4)
ALL = (0, 1, 2, 3)
FILL = {
    "inputs": [("stage", 1, ALL)],
    "n1_0": [("stage", 2, ALL)],
    "n1_3": [("cotangent", 0), ("stage", 3, ALL)],
    "kv": [("forward", 1, ALL)],
    "attend_0": [("cotangent", 1)],
    "attend_1": [("cotangent", 2), ("forward", 2, ALL), ("stage", 4, ALL)],
    "residual_0": [("cotangent", 3)],
    "residual_1": [("forward", 3, (0, 1))],
    "residual_3": [("forward", 3, (2, 3))],
    "n2_2": [("forward", 4, ALL)],
    "norm_0": [("grad", 4)],
    "norm_1": [("grad", 2)],
    "norm_2": [("reduce", 4, (0,)), ("grad", 3)],
    "norm_3": [("reduce", 4, (1, 2))],
    "ga_0": [("reduce", 4, (3,)), ("ring", 0)],
    "ga_1": [("ring", 1)],
    "ga_2": [("ring", 2)],
    "ga_3": [("ring", 3), ("reduce", 2, (0, 1))],
    "back_0": [("ring", 4), ("reduce", 2, (2, 3))],
    "back_1": [("reduce", 3, (0, 1))],
    "back_2": [("reduce", 3, (2, 3))],
    "input_0": [("reduce", 1, (0, 1))],
    "input_1": [("reduce", 1, (2, 3))],
    "end_1": [("reduce", 0, ALL)],
}


def dot(a, b, dims):
    return lax.dot_general(a, b, dims, preferred_element_type=F32)


def mod(a, n):
    return lax.rem(a, jnp.int32(n))


class Sems:
    def __init__(self):
        self.size = 0

    def take(self, count):
        first = self.size
        self.size += count
        return first


class Plan:
    def __init__(self, sizes, model, heads_cols, kv_cols, hidden_cols, tokens):
        self.YH, self.Z, self.X, self.TP = sizes
        self.n_ctx = self.YH * self.Z * self.X * 2
        self.n_dev = self.n_ctx * self.TP
        self.S = self.YH * self.X * 2
        self.YX = self.YH * self.X
        self.R = model // self.n_ctx
        self.model = model
        self.qc = heads_cols // self.Z
        self.kc = kv_cols // self.Z
        self.fc = hidden_cols // (2 * self.Z)
        self.cols = [self.qc + 2 * self.kc, self.qc, self.fc, self.fc, self.fc]
        self.half = tokens // 2
        self.rows = 2 * self.Z * self.half
        self.wide_rows = 2 * self.rows
        self.seq = self.S * self.rows
        self.nseg = self.n_ctx // 2
        self.fast = self.seq <= 2048
        self.tile = 256 if self.fast else 128
        self.tmp = 256 if self.fast else 128
        send, recv, local = Sems(), Sems(), Sems()
        W, Z, S, YX = 5, self.Z, self.S, self.YX
        self.gain_s, self.gain_r = send.take(self.n_ctx), recv.take(1)
        self.swap_s, self.swap_r = send.take(2), recv.take(2)
        self.s1_s, self.s1_r, self.s1_l = send.take(W * Z * 2), recv.take(W * Z * 2), local.take(W)
        self.s2_s, self.s2_r = send.take(W * Z * S), recv.take(W * YX * Z)
        self.ag_s, self.ag_r = send.take(4 * 5 * Z), recv.take(4 * 4 * Z)
        self.rb_s, self.rb_r = send.take(4 * CHUNKS), recv.take(4 * CHUNKS)
        self.ry_s, self.ry_r = send.take(4 * CHUNKS), recv.take(4 * CHUNKS)
        self.rz_s, self.rz_r = send.take(4 * CHUNKS * Z), recv.take(4 * CHUNKS * (Z + 1))
        self.kv_s, self.kv_r = send.take(S), recv.take(S)
        self.dkv_s, self.dkv_r = send.take(S), recv.take(S)
        self.dw_s, self.dw_r = send.take(W * self.nseg), recv.take(W * S * Z)
        self.og_s, self.og_r = send.take(W * Z * 2), recv.take(W * Z * 2)
        self.og_l = local.take(W)
        self.out_s, self.out_r, self.out_l = send.take(4), recv.take(4), local.take(2)
        self.gg_s, self.gg_r = send.take(self.n_dev), recv.take(1)
        self.tmp_l = local.take(2 * S)
        self.pack_l = local.take(3)
        self.n_send, self.n_recv, self.n_local = send.size, recv.size, local.size


def block_kernel(
    p,
    tok, cot, gin, cosr, sinr, posq, ids, wq, wk, wv, wi1, wi2, wi3, wi4,
    block_out, in_grad, gain_grad, og0, og1, og2, og3, og4, rb0, rb1, rb2, rb3, rb4,
    gbuf, swap, stq, stk, stv, pack, n1, n2, gg, ga, w0, w1, w2, w3, w4,
    qpad, gmpad, kvall, dkv, lse, ot, mixed, hid, dgate, dup, gate, up, dq, dkvr, gqkv,
    bsend, brecvs, ysend, yrecv, zsend, zrecv, acc, toks, resid, resid2, ggs, ggr, tmp,
    ssem, rsem, lsem,
):
    YH, Z, X, S, YX, R = p.YH, p.Z, p.X, p.S, p.YX, p.R
    H = p.half
    HALF = Z * H
    win = [None, wi1, wi2, wi3, wi4]
    w = [w0, w1, w2, w3, w4]
    og = [og0, og1, og2, og3, og4]
    rb = [rb0, rb1, rb2, rb3, rb4]
    yh, z, x, c, tp = (lax.axis_index(a) for a in AXES)
    sib = {"core": 1 - c}
    holder = c == tp
    other = c != tp
    ctx_of = lambda a, b, d, e: ((a * Z + b) * X + d) * 2 + e
    ctx_me = ctx_of(yh, z, x, c)
    s_me = (yh * X + x) * 2 + tp
    yx_me = yh * X + x
    zplus = lambda d: mod(z + d, Z)
    zminus = lambda d: mod(z + (Z - d), Z)
    row_of = lambda i, m: pl.multiple_of(i * m, m)
    pending = []

    def rc(src, dst, si, ri, dev):
        return pltpu.make_async_remote_copy(
            src_ref=src, dst_ref=dst, send_sem=ssem.at[si], recv_sem=rsem.at[ri],
            device_id=dev, device_id_type=MESH,
        )

    def wait_recv(dst, ri):
        rc(dst, dst, 0, ri, sib).wait_recv()

    def wait_send(src, si):
        rc(src, src, si, 0, sib).wait_send()

    def lc(src, dst, li):
        return pltpu.make_async_copy(src, dst, lsem.at[li])

    def when(pred, do):
        if pred is None:
            do()
        else:
            pl.when(pred)(do)

    def send(src, dst, si, ri, dev, pred=None):
        when(pred, lambda: rc(src, dst, si, ri, dev).start())
        pending.append(lambda: when(pred, lambda: wait_send(src, si)))

    loads = [lc(a, b, p.pack_l + n) for n, (a, b) in enumerate(((wq, stq), (wk, stk), (wv, stv)))]
    for copy in loads:
        copy.start()

    deltas = [
        (a, b, d, e, f)
        for a in range(YH) for b in range(Z) for d in range(X) for e in range(2) for f in range(p.TP)
        if a + b + d + e + f
    ]

    def away(a, b, d, e, f):
        return {
            "yh": mod(yh + a, YH), "z": mod(z + b, Z), "x": mod(x + d, X),
            "core": mod(c + e, 2), "tp": mod(tp + f, p.TP),
        }

    barrier = pltpu.get_barrier_semaphore()
    for delta in deltas:
        pl.semaphore_signal(barrier, inc=1, device_id=away(*delta), device_id_type=MESH)

    lane = lax.broadcasted_iota(jnp.int32, (1, 128), 1)
    low = lane < HEAD_DIM
    for copy in loads:
        copy.wait()
    for b in range(Z):
        pack[b, :, 0 : p.qc] = stq[:, b * p.qc : (b + 1) * p.qc]
        both = slice(b // 2 * 128, b // 2 * 128 + 128)
        key, val = stk[:, both].astype(F32), stv[:, both].astype(F32)
        if b % 2:
            pair = jnp.where(low, pltpu.roll(key, 64, 1), val)
        else:
            pair = jnp.where(low, key, pltpu.roll(val, 64, 1))
        pack[b, :, p.qc : p.qc + 128] = pair.astype(BF16)
    pl.semaphore_wait(barrier, len(deltas))

    gain_peers = [d for d in deltas if d[4] == 0]
    gbuf[ctx_me] = gin[...]
    for n, src in enumerate((tok, cot)):
        send(src.at[pl.ds(row_of(1 - c, H), H)], swap.at[n], p.swap_s + n, p.swap_r + n, sib)
    for n, delta in enumerate(gain_peers):
        send(gin, gbuf.at[ctx_me], p.gain_s + n, p.gain_r, away(*delta))

    def seg(a, b, d):
        return pl.ds(pl.multiple_of(ctx_of(a, b, d, 0) * R, 2 * R), 2 * R)

    def block(a, b, d, e):
        return pl.ds(pl.multiple_of(ctx_of(a, b, d, e) * R, R), R)

    def piece(i, zz, cc):
        if i == 0:
            return pack.at[zz]
        n = p.cols[i]
        return win[i].at[:, pl.ds(row_of(zz * 2 + cc if i in WIDE else zz, n), n)]

    def s1r(i, d, e):
        return p.s1_r + (i * Z + d) * 2 + e

    def w_stage1(i, steps=None):
        dst = w[i].at[block(yh, z, x, c)]
        for d in range(Z) if steps is None else steps:
            si = p.s1_s + (i * Z + d) * 2
            if i in WIDE:
                for e in range(2):
                    src = piece(i, zplus(d), mod(c + e, 2))
                    if d + e:
                        send(src, dst, si + e, s1r(i, d, c), {"z": zplus(d), "core": mod(c + e, 2)})
                    else:
                        lc(src, dst, p.s1_l + i).start()
                continue
            src = piece(i, zplus(d), c)
            if d == 0:
                pl.when(holder)(lambda: lc(src, dst, p.s1_l + i).start())
            send(src, dst, si, s1r(i, d, c), {"z": zplus(d), "core": tp}, other if d == 0 else None)

    plane = [(a, d, f) for a in range(YH) for d in range(X) for f in range(2) if a + d + f]
    line = [(a, d) for a in range(YH) for d in range(X) if a + d]

    def w_forward(i, steps=None):
        def arrived(d):
            zs = zminus(d)
            if d == 0:
                lc(piece(i, z, c), w[i].at[block(yh, z, x, c)], p.s1_l + i).wait()
                wait_recv(w[i].at[block(yh, z, x, 1 - c)], s1r(i, 0, 1 - c))
            else:
                for e in range(2):
                    wait_recv(w[i].at[block(yh, zs, x, e)], s1r(i, d, e))

        for d in range(Z) if steps is None else steps:
            when(None if i in WIDE else holder, lambda: arrived(d))
            part = w[i].at[seg(yh, zminus(d), x)]
            for n, peer in enumerate(line if i in WIDE else plane):
                send(
                    part, part, p.s2_s + (i * Z + d) * S + n,
                    p.s2_r + (i * YX + peer[0] * X + peer[1]) * Z + d,
                    away(peer[0], 0, peer[1], 0, 0 if i in WIDE else peer[2]),
                    None if i in WIDE else holder,
                )

    def w_wait(i):
        for a in range(YH):
            for dx in range(X):
                def wait_all():
                    for d in range(Z):
                        part = w[i].at[seg(mod(yh + YH - a, YH), zminus(d), mod(x + X - dx, X))]
                        wait_recv(part, p.s2_r + (i * YX + a * X + dx) * Z + d)
                if a + dx:
                    wait_all()
                elif i not in WIDE:
                    pl.when(other)(wait_all)

    def rows_at(g, e, b):
        return pl.ds(pl.multiple_of(((g * 2 + e) * Z + b) * H, H), H)

    up_z, down_z = jnp.minimum(z + 1, Z - 1), jnp.maximum(z - 1, 0)

    def ag_step(k, buf, dist, wide):
        g = tp if wide else 0
        rbase, sbase = p.ag_r + k * 4 * Z, p.ag_s + k * 5 * Z
        if dist == 0:
            mine = buf.at[rows_at(g, c, z)]
            send(mine, mine, sbase + z, rbase + z, {"z": up_z}, z < Z - 1)
            send(mine, mine, sbase + 4 * Z + z, rbase + z, {"z": down_z}, z > 0)
            send(mine, mine, sbase + Z + z, rbase + Z + z, sib)
            if wide:
                send(mine, mine, sbase + 2 * Z + z, rbase + 2 * Z + z, {"tp": 1 - tp})
            return
        for sign in (-1, 1):
            there = z + sign * dist
            has = (there >= 0) & (there < Z)
            b = jnp.clip(there, 0, Z - 1)
            part = buf.at[rows_at(g, c, b)]
            pl.when(has)(lambda: wait_recv(part, rbase + b))
            if dist < Z - 1:
                if sign < 0:
                    send(part, part, sbase + b, rbase + b, {"z": up_z}, has & (z < Z - 1))
                else:
                    send(part, part, sbase + b, rbase + b, {"z": down_z}, has & (z > 0))
            send(part, part, sbase + Z + b, rbase + Z + b, sib, has)
            if wide:
                send(part, part, sbase + 2 * Z + b, rbase + 2 * Z + b, {"tp": 1 - tp}, has)

    def ag_tail(k, buf, wide):
        g = tp if wide else 0
        rbase, sbase = p.ag_r + k * 4 * Z, p.ag_s + k * 5 * Z
        for b in range(Z):
            wait_recv(buf.at[rows_at(g, 1 - c, b)], rbase + Z + b)
        if not wide:
            return
        for b in range(Z):
            part = buf.at[rows_at(1 - tp, c, b)]
            wait_recv(part, rbase + 2 * Z + b)
            send(part, part, sbase + 3 * Z + b, rbase + 3 * Z + b, sib)
        for b in range(Z):
            wait_recv(buf.at[rows_at(1 - tp, 1 - c, b)], rbase + 3 * Z + b)

    def gather(k, buf, wide):
        for dist in range(1, Z):
            ag_step(k, buf, dist, wide)
        ag_tail(k, buf, wide)

    CW = p.model // CHUNKS
    used = {}

    def reuse(name, k):
        before = used.get(name)
        used[name] = k
        return before

    def brecv(k):
        return brecvs.at[0 if k == 1 else 1]

    def groups(k):
        return 2 if k in (1, 2) else 1

    def bsent(k, j):
        wait_send(bsend.at[j, pl.ds(0, groups(k))], p.rb_s + k * CHUNKS + j)

    def ysent(k, j):
        wait_send(ysend.at[j], p.ry_s + k * CHUNKS + j)

    def product(terms, j, g, e):
        rows = pl.ds(pl.multiple_of((g * 2 + e) * HALF, HALF), HALF)
        cols = pl.ds(pl.multiple_of(j * CW, CW), CW)
        total = None
        for a, b in terms:
            part = dot(a[rows, :], b[cols, :], NT)
            total = part if total is None else total + part
        return total

    def own_at(j):
        return pl.ds(pl.multiple_of(j * HALF, HALF), HALF)

    def owns(k):
        return up if k == 2 else gate

    def rs_parts(k, terms):
        wide = groups(k) == 2
        mine = tp if wide else 0
        before_b = reuse("b", k)
        before_y = reuse("y", k) if wide else None

        def first(j, carry):
            values = [product(terms, j, g, 1 - c).astype(BF16) for g in range(groups(k))]
            if before_b is not None:
                bsent(before_b, j)
            for g, value in enumerate(values):
                bsend[j, g] = value
            rc(
                bsend.at[j, pl.ds(0, groups(k))], brecv(k).at[j, pl.ds(0, groups(k))],
                p.rb_s + k * CHUNKS + j, p.rb_r + k * CHUNKS + j, sib,
            ).start()
            return carry

        lax.fori_loop(0, CHUNKS, first, 0)

        def second(j, carry):
            value = product(terms, j, 1 - tp, c) if wide else None
            wait_recv(brecv(k).at[j, pl.ds(0, groups(k))], p.rb_r + k * CHUNKS + j)
            owns(k)[own_at(j), :] = product(terms, j, mine, c) + brecv(k)[j, mine].astype(F32)
            if not wide:
                return carry
            if before_y is not None:
                ysent(before_y, j)
            ysend[j] = (value + brecv(k)[j, 1 - tp].astype(F32)).astype(BF16)
            rc(
                ysend.at[j], yrecv.at[k - 1, j], p.ry_s + k * CHUNKS + j, p.ry_r + k * CHUNKS + j, {"tp": 1 - tp}
            ).start()
            return carry

        lax.fori_loop(0, CHUNKS, second, 0)

    def rz_r(k, j, t):
        return p.rz_r + (k * CHUNKS + j) * (Z + 1) + t

    def zsent(k, j, t):
        wait_send(zsend.at[j, t], p.rz_s + (k * CHUNKS + j) * Z + t)

    def zslot(k):
        return zrecv.at[k % 3]

    def add_y(k, j):
        if groups(k) == 2:
            wait_recv(yrecv.at[k - 1, j], p.ry_r + k * CHUNKS + j)
            owns(k)[own_at(j), :] += yrecv[k - 1, j].astype(F32)

    rings = {}

    def ring_step(k, step):
        if step == 0:
            rings[k] = reuse("z", k)
        before = rings[k]

        def move(j, t, near):
            upward = z < t
            has = jnp.where(upward, z > 0, z < Z - 1)
            mine = owns(k).at[pl.ds(j * HALF + t * H, H)]

            @pl.when((z != t) & (jnp.where(upward, z < Z // 2, z >= Z // 2) == near))
            def _():
                if before is not None:
                    zsent(before, j, t)

                @pl.when(has)
                def _():
                    wait_recv(zslot(k).at[j, t], rz_r(k, j, t))
                    zsend[j, t] = (mine[...] + zslot(k)[j, t].astype(F32)).astype(BF16)

                @pl.when(jnp.logical_not(has))
                def _():
                    zsend[j, t] = mine[...].astype(BF16)

                to = jnp.where(upward, up_z, down_z)
                slot = jnp.where((to == t) & jnp.logical_not(upward), Z, t)
                rc(
                    zsend.at[j, t], zslot(k).at[j, slot],
                    p.rz_s + (k * CHUNKS + j) * Z + t, rz_r(k, j, slot), {"z": to},
                ).start()

        order = (Z - 1, 0, *range(Z - 2, 0, -1))
        if step < CHUNKS:
            add_y(k, step)
            for t in order:
                move(step, t, True)
        if step:
            for t in order:
                move(step - 1, t, False)

    def rs_ring(k, between):
        for step in range(CHUNKS + 1):
            ring_step(k, step)
            if step < CHUNKS:
                between(step)

    def rs_finish(k):
        for j in range(CHUNKS):
            cols = slice(j * CW, (j + 1) * CW)
            acc[:, cols] = owns(k)[pl.ds(pl.multiple_of(j * HALF + z * H, H), H), :]

            @pl.when(z > 0)
            def _():
                wait_recv(zslot(k).at[j, z], rz_r(k, j, z))
                acc[:, cols] += zslot(k)[j, z].astype(F32)

            @pl.when(z < Z - 1)
            def _():
                wait_recv(zslot(k).at[j, Z], rz_r(k, j, Z))
                acc[:, cols] += zslot(k)[j, Z].astype(F32)
        return acc[...]

    per = 256 // (2 * R)

    def dw_place(i, g):
        xd, zd, yd = mod(g, X), mod(lax.div(g, jnp.int32(X)), Z), lax.div(g, jnp.int32(X * Z))
        mine = (xd == x) & (yd == yh)
        return xd, zd, yd, mine if i in WIDE else mine & holder

    def dw_send(i, rows_ref, grad):
        def one(t, carry):
            cols = pl.ds(pl.multiple_of(t * 256, 256), 256)
            w[i][cols, :] = dot(rows_ref[:, cols], grad[...], TN).astype(BF16)
            for n in range(per):
                g = t * per + n
                xd, zd, yd, mine = dw_place(i, g)
                from_me = yx_me if i in WIDE else s_me

                @pl.when(jnp.logical_not(mine))
                def _():
                    rc(
                        w[i].at[pl.ds(pl.multiple_of(g * 2 * R, 2 * R), 2 * R)], rb[i].at[from_me, zd],
                        p.dw_s + i * p.nseg + g, p.dw_r + (i * S + from_me) * Z + zd,
                        {"yh": yd, "x": xd, "tp": tp if i in WIDE else c},
                    ).start()
            return carry

        lax.fori_loop(0, p.model // 256, one, 0)

    def dw_sent(i):
        for g in range(p.nseg):
            mine = dw_place(i, jnp.int32(g))[3]

            @pl.when(jnp.logical_not(mine))
            def _():
                wait_send(w[i].at[pl.ds(g * 2 * R, 2 * R)], p.dw_s + i * p.nseg + g)

    def place(i, zz, cc):
        if i == 0:
            return og[0].at[zz]
        n = p.cols[i]
        return og[i].at[:, pl.ds(row_of(zz * 2 + cc if i in WIDE else zz, n), n)]

    def ogr(i, zz, cc):
        return p.og_r + (i * Z + zz) * 2 + (cc if i in WIDE else 0)

    def dw_reduce(i, zds=None):
        n = p.cols[i]
        size, me = (YX, yx_me) if i in WIDE else (S, s_me)
        items = [(zd, at, min(p.tmp, n - at)) for zd in (range(Z) if zds is None else zds) for at in range(0, n, p.tmp)]

        def tiles(q):
            zd, at, width = items[q]
            return [
                lc(
                    rb[i].at[mod(me + d, size), zd, :, pl.ds(at, width)],
                    tmp.at[q % 2, d - 1, :, pl.ds(0, width)], p.tmp_l + q % 2 * S + d,
                )
                for d in range(1, size)
            ]

        def begin(q):
            zd, at, _ = items[q]
            if at == 0:
                for d in range(1, size):
                    s = mod(me + d, size)
                    wait_recv(rb[i].at[s, zd], p.dw_r + (i * S + s) * Z + zd)
            for copy in tiles(q):
                copy.start()

        def run():
            begin(0)
            for q, (zd, at, width) in enumerate(items):
                if q + 1 < len(items):
                    begin(q + 1)
                for copy in tiles(q):
                    copy.wait()
                mine = seg(yh, zd, x)
                total = w[i][mine, at : at + width].astype(F32)
                for d in range(1, size):
                    total = total + tmp[q % 2, d - 1, :, 0:width].astype(F32)
                w[i][mine, at : at + width] = total.astype(BF16)
                if at + width < n:
                    continue
                for e in range(2):
                    src = w[i].at[block(yh, zd, x, e)]
                    here = (z == zd) & (c == e)

                    @pl.when(here)
                    def _():
                        lc(src, place(i, z, c), p.og_l + i).start()

                    @pl.when(jnp.logical_not(here))
                    def _():
                        rc(
                            src, place(i, z, c), p.og_s + (i * Z + zd) * 2 + e, ogr(i, z, c),
                            {"z": jnp.int32(zd), "core": jnp.int32(e)},
                        ).start()

        when(None if i in WIDE else holder, run)

    def dw_done(i):
        cores = range(2) if i in WIDE else (0,)
        for b in range(Z):
            for e in cores:
                here = (z == b) & ((c == e) if i in WIDE else holder)

                @pl.when(here)
                def _():
                    lc(w[i].at[block(yh, z, x, c)], place(i, z, c), p.og_l + i).wait()

                @pl.when(jnp.logical_not(here))
                def _():
                    wait_recv(place(i, jnp.int32(b), jnp.int32(e)), ogr(i, b, e))

        def sent():
            for zd in range(Z):
                for e in range(2):
                    @pl.when(jnp.logical_not((z == zd) & (c == e)))
                    def _():
                        wait_send(w[i].at[block(yh, zd, x, e)], p.og_s + (i * Z + zd) * 2 + e)

        when(None if i in WIDE else holder, sent)

    def deliver(k, out):
        dst = out.at[pl.ds(row_of(c, H), H)]
        for t in range(p.TP):
            here = holder & (tp == t)
            pl.when(here)(lambda: lc(swap.at[k], dst, p.out_l + k).start())
            send(
                swap.at[k], dst, p.out_s + k * 2 + t, p.out_r + k * 2 + c,
                {"core": tp, "tp": jnp.int32(t)}, jnp.logical_not(here),
            )

    def delivered(k, out):
        for e in range(2):
            here = holder & (c == e)

            @pl.when(here)
            def _():
                lc(swap.at[k], out.at[pl.ds(row_of(c, H), H)], p.out_l + k).wait()

            @pl.when(jnp.logical_not(here))
            def _():
                wait_recv(out.at[pl.ds(e * H, H)], p.out_r + k * 2 + e)

    def fill(point):
        for kind, *args in FILL.get(point, ()):
            if kind == "stage":
                w_stage1(args[0], args[1])
            elif kind == "forward":
                w_forward(args[0], args[1])
            elif kind == "cotangent":
                ag_step(1, gg, args[0], True)
            elif kind == "ring":
                ring_step(2, args[0])
            elif kind == "grad":
                dw_send(args[0], gg if args[0] == 4 else n2, {4: hid, 2: dgate, 3: dup}[args[0]])
            else:
                dw_reduce(args[0], args[1])

    w_stage1(0)
    for n in range(2):
        wait_recv(swap.at[n], p.swap_r + n)
    mine = pl.ds(row_of(c, H), H)
    toks[...] = jnp.where(holder, tok[mine, :], swap[0])
    gg[rows_at(tp, c, z), :] = jnp.where(holder, cot[mine, :], swap[1])
    token_rows = toks[...].astype(F32)
    fill("inputs")
    factor_attn = lax.rsqrt(jnp.mean(token_rows * token_rows, axis=1, keepdims=True) + EPS)
    wait_recv(gbuf.at[pl.ds(0, p.n_ctx - 1)], p.gain_r)
    q = p.n_ctx * 128 // p.model
    gain_parts = []
    for b in range(p.model // 128):
        total = gbuf[b * q]
        for n in range(1, q):
            total = total + gbuf[b * q + n]
        gain_parts.append(total)
    gains = jnp.concatenate(gain_parts, axis=1)
    gain_attn, gain_mlp = gains[0:1, :], gains[1:2, :]
    n1[rows_at(0, c, z), :] = (token_rows * factor_attn * gain_attn).astype(BF16)
    ag_step(0, n1, 0, False)
    fill("n1_0")
    w_forward(0)
    ag_step(0, n1, 1, False)
    fill("n1_1")
    ag_step(0, n1, 2, False)
    fill("n1_2")
    ag_step(0, n1, 3, False)
    ag_tail(0, n1, False)
    fill("n1_3")
    w_wait(0)

    first_half = mod(lane, HEAD_DIM) < HEAD_DIM // 2

    def rotate(t, cosine, sine):
        turned = jnp.where(first_half, pltpu.roll(t, 96, 1), pltpu.roll(t, 32, 1))
        return t * cosine + turned * sine

    lin = dot(n1[...], w0[...], NN)
    cosine, sine = cosr[...], sinr[...]
    scale = HEAD_DIM ** (-0.5)
    pairs = p.qc // 128
    kv_lin = lin[:, p.qc : p.qc + 128]
    own_rows = pl.ds(pl.multiple_of(s_me * p.rows, p.rows), p.rows)
    kvall[own_rows, :] = jnp.where(low, rotate(kv_lin, cosine, sine), kv_lin).astype(BF16)
    for n, (a, dx, f) in enumerate(plane):
        send(kvall.at[own_rows], kvall.at[own_rows], p.kv_s + n, p.kv_r + n, away(a, 0, dx, 0, f))
    for n in range(pairs):
        turned_q = rotate(lin[:, n * 128 : (n + 1) * 128], cosine, sine).astype(BF16).astype(F32) * scale
        qpad[2 * n] = jnp.where(low, turned_q, 0.0).astype(BF16)
        qpad[2 * n + 1] = jnp.where(low, pltpu.roll(turned_q, 64, 1), 0.0).astype(BF16)

    def from_plane(a, dx, f):
        s = (mod(yh + YH - a, YH) * X + mod(x + X - dx, X)) * 2 + mod(tp + 2 - f, 2)
        return pl.ds(pl.multiple_of(s * p.rows, p.rows), p.rows)

    fill("kv")
    for n, delta in enumerate(plane):
        wait_recv(kvall.at[from_plane(*delta)], p.kv_r + n)
    fill("attend_0")
    T = p.tile
    KC = p.rows
    down = lax.broadcasted_iota(jnp.int32, (BLOCK, 1), 0)

    def masked(s, rows, scores):
        at = posq[:, rows]
        parts = []
        for b in range(2 * Z):
            allowed = down <= at - ids[s, b] * BLOCK
            parts.append(jnp.where(allowed, scores[b * BLOCK : (b + 1) * BLOCK, :], NEG))
        return jnp.concatenate(parts, axis=0)

    def keys(s):
        return pl.ds(s * KC, KC)

    for n in range(pairs):
        def attend(t, carry):
            rows = pl.ds(pl.multiple_of(t * T, T), T)
            outs = []
            for e in range(2):
                h = 2 * n + e
                query = qpad[h, rows, :]
                top = jnp.full((8, T), NEG, F32)
                for s in range(S):
                    scores = masked(s, rows, dot(kvall[keys(s), :], query, NT))
                    dkv[keys(s), :] = scores
                    top = jnp.maximum(top, jnp.max(scores.reshape(KC // 8, 8, T), axis=0))
                top = jnp.max(top, axis=0, keepdims=True)
                total = jnp.zeros((8, T), F32)
                for s in range(S):
                    grown = jnp.exp(dkv[keys(s), :] - top)
                    dkv[keys(s), :] = grown
                    total = total + jnp.sum(grown.reshape(KC // 8, 8, T), axis=0)
                total = jnp.sum(total, axis=0, keepdims=True)
                lse[h : h + 1, rows] = top + jnp.log(total)
                share = 1.0 / total
                out = jnp.zeros((128, T), F32)
                for s in range(S):
                    out = out + dot(kvall[keys(s), :], (dkv[keys(s), :] * share).astype(BF16), TN)
                outs.append(out[HEAD_DIM:, :])
            out = jnp.concatenate(outs, axis=0)
            ot[n, :, rows] = out
            mixed[rows, n * 128 : (n + 1) * 128] = jnp.transpose(out).astype(BF16)
            return carry

        lax.fori_loop(0, p.rows // T, attend, 0)
        fill(f"attend_{n + 1}")
    w_wait(1)
    rs_parts(0, [(mixed, w1)])
    rs_ring(0, lambda j: fill(f"residual_{j}"))
    residual = toks[...].astype(F32) + rs_finish(0)
    resid[...] = residual
    factor_mlp = lax.rsqrt(jnp.mean(residual * residual, axis=1, keepdims=True) + EPS)
    n2[rows_at(tp, c, z), :] = (residual * factor_mlp * gain_mlp).astype(BF16)
    ag_step(2, n2, 0, True)
    fill("n2_0")
    ag_step(2, n2, 1, True)
    fill("n2_1")
    ag_step(2, n2, 2, True)
    fill("n2_2")
    ag_step(2, n2, 3, True)
    ag_tail(2, n2, True)
    fill("n2_3")

    w_wait(2)
    w_wait(3)

    def feed(t, carry):
        cols = pl.ds(pl.multiple_of(t * 256, 256), 256)
        gate[:, cols] = dot(n2[...], w2[:, cols], NN)
        up[:, cols] = dot(n2[...], w3[:, cols], NN)
        return carry

    lax.fori_loop(0, p.fc // 256, feed, 0)
    fill("feed")
    ag_tail(1, gg, True)
    w_wait(4)

    def feed_back(t, carry):
        cols = pl.ds(pl.multiple_of(t * 256, 256), 256)
        back = dot(gg[...], w4[:, cols], NN)
        gate_pre, up_pre = gate[:, cols], up[:, cols]
        sig = jax.nn.sigmoid(gate_pre)
        silu = gate_pre * sig
        hid[:, cols] = (silu * up_pre).astype(BF16)
        dgate[:, cols] = (back * up_pre * sig * (1.0 + gate_pre * (1.0 - sig))).astype(BF16)
        dup[:, cols] = (back * silu).astype(BF16)
        return carry

    lax.fori_loop(0, p.fc // 256, feed_back, 0)
    drain = pending[:]
    pending.clear()
    for wait in drain:
        wait()
    norm_terms, out_terms = [(dgate, w2), (dup, w3)], [(hid, w4)]
    rs_parts(1, norm_terms)
    rs_parts(2, out_terms)
    rs_ring(1, lambda j: fill(f"norm_{j}"))
    grad_norm_mlp = rs_finish(1)
    weighted = grad_norm_mlp * gain_mlp
    u = resid[...] * factor_mlp
    grad_residual = gg[rows_at(tp, c, z), :].astype(F32) + factor_mlp * (
        weighted - u * jnp.mean(weighted * u, axis=1, keepdims=True)
    )
    gain_mlp_part = jnp.sum(grad_norm_mlp * u, axis=0, keepdims=True)
    ga[rows_at(0, c, z), :] = grad_residual.astype(BF16)
    resid2[...] = grad_residual
    ag_step(3, ga, 0, False)
    fill("ga_0")
    ag_step(3, ga, 1, False)
    fill("ga_1")
    ag_step(3, ga, 2, False)
    fill("ga_2")
    ag_step(3, ga, 3, False)
    ag_tail(3, ga, False)
    fill("ga_3")

    for n in range(pairs):
        gm = dot(ga[...], w1[:, n * 128 : (n + 1) * 128], NN).astype(BF16).astype(F32)
        ot[n] = ot[n] * jnp.transpose(gm)
        gmpad[2 * n] = jnp.where(low, 0.0, pltpu.roll(gm, 64, 1)).astype(BF16)
        gmpad[2 * n + 1] = jnp.where(low, 0.0, gm).astype(BF16)
    dw_send(1, ga, mixed)
    fill("back_0")
    dkv[:, 0:128] = jnp.zeros((p.seq, 128), F32)
    for n in range(pairs):
        def attend_back(t, carry):
            rows = pl.ds(pl.multiple_of(t * T, T), T)
            agree = ot[n, :, rows]
            outs = []
            for e in range(2):
                h = 2 * n + e
                query, back = qpad[h, rows, :], gmpad[h, rows, :]
                level = lse[h : h + 1, rows]
                delta = jnp.sum(agree[e * HEAD_DIM : (e + 1) * HEAD_DIM, :], axis=0, keepdims=True)
                out = jnp.zeros((128, T), F32)
                for s in range(S):
                    here = kvall[keys(s), :]
                    probs = jnp.exp(masked(s, rows, dot(here, query, NT)) - level)
                    ds = (probs * (dot(here, back, NT) - delta)).astype(BF16)
                    out = out + dot(here, ds, TN)
                    dkv[keys(s), 0:128] += dot(ds, query, NN) + dot(probs.astype(BF16), back, NN)
                outs.append(out[:HEAD_DIM, :])
            dq[rows, n * 128 : (n + 1) * 128] = jnp.transpose(jnp.concatenate(outs, axis=0)) * scale
            return carry

        lax.fori_loop(0, p.rows // T, attend_back, 0)
        fill(f"back_{n + 1}")
    dkv_own = dkv[own_rows, 0:128]
    for s in range(S):
        kvall[keys(s), :] = dkv[keys(s), 0:128].astype(BF16)
    for n, (a, dx, f) in enumerate(plane):
        s = (mod(yh + a, YH) * X + mod(x + dx, X)) * 2 + mod(tp + f, 2)
        send(
            kvall.at[pl.ds(pl.multiple_of(s * p.rows, p.rows), p.rows)], dkvr.at[n],
            p.dkv_s + n, p.dkv_r + n, away(a, 0, dx, 0, f),
        )
    fill("terms")
    for n in range(pairs):
        cols = slice(n * 128, (n + 1) * 128)
        gqkv[:, cols] = rotate(dq[:, cols], cosr[...], -sinr[...]).astype(BF16)
    for n in range(len(plane)):
        wait_recv(dkvr.at[n], p.dkv_r + n)
        dkv_own = dkv_own + dkvr[n].astype(F32)
    gqkv[:, p.qc : p.qc + 128] = jnp.where(low, rotate(dkv_own, cosr[...], -sinr[...]), dkv_own).astype(BF16)
    rs_parts(3, [(gqkv, w0)])
    dw_send(0, n1, gqkv)
    rs_ring(3, lambda j: fill(f"input_{j}"))
    grad_norm_attn = rs_finish(3)
    weighted = grad_norm_attn * gain_attn
    scaled_attn = toks[...].astype(F32) * factor_attn
    swap[1] = (
        resid2[...] + factor_attn * (weighted - scaled_attn * jnp.mean(weighted * scaled_attn, axis=1, keepdims=True))
    ).astype(BF16)
    deliver(1, in_grad)

    gain_attn_part = jnp.sum(grad_norm_attn * scaled_attn, axis=0, keepdims=True)
    both_gains = jnp.concatenate([gain_attn_part, gain_mlp_part, jnp.zeros((6, p.model), F32)], axis=0)
    for b in range(p.model // 128):
        ggs[b] = both_gains[:, b * 128 : (b + 1) * 128]
    dev_me = ctx_me * p.TP + tp
    ggr[dev_me] = ggs[lax.div(ctx_me * R, jnp.int32(128))]
    for n, delta in enumerate(deltas):
        to = away(*delta)
        there = ctx_of(to["yh"], to["z"], to["x"], to["core"])
        send(ggs.at[lax.div(there * R, jnp.int32(128))], ggr.at[dev_me], p.gg_s + n, p.gg_r, to)

    fill("end_0")
    swap[0] = (resid[...] + rs_finish(2)).astype(BF16)
    deliver(0, block_out)
    fill("end_1")
    wait_recv(ggr.at[pl.ds(0, p.n_dev - 1)], p.gg_r)
    total = ggr[0]
    for n in range(1, p.n_dev):
        total = total + ggr[n]
    gain_grad[...] = total

    for i in (4, 2, 3, 1, 0):
        dw_sent(i)
        dw_done(i)
    delivered(0, block_out)
    delivered(1, in_grad)
    for wait in pending:
        wait()

    def last(j, carry):
        bsent(3, j)
        ysent(2, j)
        for t in range(Z):
            pl.when(z != t)(lambda: zsent(used["z"], j, t))
        return carry

    lax.fori_loop(0, CHUNKS, last, 0)


def unpack_kernel(
    p, g0, g1, g2, g3, g4, rows0, rows1, o_q, o_k, o_v, o1, o2, o3, o4, out0, out1,
    s0, s1, s2, s3, s4, s5, s6, t_q, t_k, t_v, t1, t2, t3, t4, sem,
):
    copies = []
    pairs = [(g0, s0), (g2, s2), (g3, s3), (g4, s4), (g1, s1), (rows0, s5), (rows1, s6)]
    loads = [pltpu.make_async_copy(a, b, sem.at[n]) for n, (a, b) in enumerate(pairs)]
    for copy in loads:
        copy.start()

    def store(src, dst, n):
        copy = pltpu.make_async_copy(src, dst, sem.at[7 + n])
        copy.start()
        copies.append(copy)

    loads[0].wait()
    low = lax.broadcasted_iota(jnp.int32, (1, 128), 1) < HEAD_DIM
    for b in range(p.Z):
        t_q[:, b * p.qc : (b + 1) * p.qc] = s0[b, :, 0 : p.qc].astype(F32)
    for b in range(0, p.Z, 2):
        one, two = (s0[b + n, :, p.qc : p.qc + 128].astype(F32) for n in range(2))
        both = slice(b * HEAD_DIM, b * HEAD_DIM + 128)
        t_k[:, both] = jnp.where(low, one, pltpu.roll(two, 64, 1))
        t_v[:, both] = jnp.where(low, pltpu.roll(one, 64, 1), two)
    for n, (t, o) in enumerate(((t_q, o_q), (t_k, o_k), (t_v, o_v))):
        store(t, o, n)
    for n, (src, t, o) in enumerate(((s2, t2, o2), (s3, t3, o3), (s4, t4, o4), (s1, t1, o1))):
        loads[n + 1].wait()
        t[...] = src[...].astype(F32)
        store(t, o, n + 3)
    for n, (src, o) in enumerate(((s5, out0), (s6, out1))):
        loads[n + 5].wait()
        store(src, o, n + 7)
    for copy in copies:
        copy.wait()


def local(sizes, tokens, block_ids, gain_attn, w_query, key_weight, value_weight, w_out, gain_mlp,
          w_gate, w_up, w_down, cotangent):
    row_count, model = tokens.shape
    p = Plan(sizes, model, w_query.shape[1], key_weight.shape[1], w_gate.shape[1], row_count)
    YH, Z, X, S, R = p.YH, p.Z, p.X, p.S, p.R
    yh, z, x, c, tp = (lax.axis_index(a) for a in AXES)
    ctx_me = ((yh * Z + z) * X + x) * 2 + c
    s_me = (yh * X + x) * 2 + tp
    ids = block_ids.reshape(YH, Z, X, 2, 2).transpose(0, 2, 3, 4, 1).reshape(S, 2 * Z)
    positions = (ids[:, :, None] * BLOCK + jnp.arange(BLOCK, dtype=jnp.int32)).reshape(S, p.rows)
    own = lax.dynamic_slice_in_dim(positions, s_me, 1, 0)
    half = HEAD_DIM // 2
    frequencies = THETA ** (-(jnp.arange(half, dtype=F32) * 2.0 / HEAD_DIM))
    angles = own.reshape(p.rows, 1).astype(F32) * jnp.tile(frequencies, 4)[None, :]
    signs = jnp.where(jnp.arange(128) % HEAD_DIM < half, -1.0, 1.0).astype(F32)
    cosine, sine = jnp.cos(angles), jnp.sin(angles) * signs
    gains = jnp.stack([gain_attn, gain_mlp]).astype(F32)
    gin = lax.dynamic_update_slice(jnp.zeros((8, 128), F32), gains, (0, lax.rem(ctx_me * R, 128)))
    V = pl.BlockSpec(memory_space=pltpu.VMEM)
    A = pl.BlockSpec(memory_space=pl.ANY)
    H = p.half
    sd = jax.ShapeDtypeStruct
    out_shape = [sd((row_count, model), BF16), sd((row_count, model), BF16), sd((8, 128), F32)]
    out_shape += [sd((Z, R, p.cols[0]), BF16), sd(w_out.shape, BF16)] + [sd(w_gate.shape, BF16)] * 3
    out_shape += [sd((p.YX if i in WIDE else S, Z, 2 * R, n), BF16) for i, n in enumerate(p.cols)]
    CW = model // CHUNKS
    assert CW == p.fc and CHUNKS * Z * H == p.wide_rows
    scratch = [
        pltpu.VMEM((p.n_ctx, 8, 128), F32),
        pltpu.VMEM((2, H, model), BF16),
        *[pltpu.VMEM(a.shape, BF16) for a in (w_query, key_weight, value_weight)],
        pltpu.VMEM((Z, R, p.cols[0]), BF16),
        *[pltpu.VMEM((n, model), BF16) for n in (p.rows, p.wide_rows, p.wide_rows, p.rows)],
        *[pltpu.VMEM((model, n), BF16) for n in p.cols],
        pltpu.VMEM((p.qc // 64, p.rows, 128), BF16),
        pltpu.VMEM((p.qc // 64, p.rows, 128), BF16),
        pltpu.VMEM((p.seq, 128), BF16),
        pltpu.VMEM((p.seq, p.tile), F32),
        pltpu.VMEM((8, p.rows), F32),
        pltpu.VMEM((p.qc // 128, 128, p.rows), F32),
        pltpu.VMEM((p.rows, p.qc), BF16),
        *[pltpu.VMEM((p.wide_rows, p.fc), BF16) for _ in range(3)],
        *[pltpu.VMEM((p.wide_rows, p.fc), F32) for _ in range(2)],
        pltpu.VMEM((p.rows, p.qc), F32),
        pltpu.VMEM((S - 1, p.rows, 128), BF16),
        pltpu.VMEM((p.rows, p.cols[0]), BF16),
        pltpu.VMEM((CHUNKS, 2, Z * H, CW), BF16),
        pltpu.VMEM((2, CHUNKS, 2, Z * H, CW), BF16),
        pltpu.VMEM((CHUNKS, Z * H, CW), BF16),
        pltpu.VMEM((2, CHUNKS, Z * H, CW), BF16),
        pltpu.VMEM((CHUNKS, Z, H, CW), BF16),
        pltpu.VMEM((3, CHUNKS, Z + 1, H, CW), BF16),
        pltpu.VMEM((H, model), F32),
        pltpu.VMEM((H, model), BF16),
        pltpu.VMEM((H, model), F32),
        pltpu.VMEM((H, model), F32),
        pltpu.VMEM((model // 128, 8, 128), F32),
        pltpu.VMEM((p.n_dev, 8, 128), F32),
        pltpu.VMEM((2, S - 1, 2 * R, p.tmp), BF16),
        pltpu.SemaphoreType.DMA((p.n_send,)),
        pltpu.SemaphoreType.DMA((p.n_recv,)),
        pltpu.SemaphoreType.DMA((p.n_local,)),
    ]
    outs = pl.pallas_call(
        lambda *refs: block_kernel(p, *refs),
        out_shape=out_shape,
        in_specs=[V] * 6 + [pl.BlockSpec(memory_space=pltpu.SMEM)] + [A] * 7,
        out_specs=[A, A, V] + [A] * 10,
        scratch_shapes=scratch,
        compiler_params=pltpu.CompilerParams(
            collective_id=0, has_side_effects=True, vmem_limit_bytes=65400 * 1024
        ),
        name="block",
    )(
        tokens, cotangent, gin, cosine, sine, own, ids,
        w_query, key_weight, value_weight, w_out, w_gate, w_up, w_down,
    )
    gain_grad, grads = outs[2], list(outs[3:8])
    shapes = [a.shape for a in (w_query, key_weight, value_weight, w_out, w_gate, w_up, w_down)]
    unpacked = pl.pallas_call(
        lambda *refs: unpack_kernel(p, *refs),
        out_shape=[sd(a, F32) for a in shapes] + [sd((row_count, model), BF16)] * 2,
        in_specs=[A] * 7,
        out_specs=[A] * 9,
        scratch_shapes=[
            *[pltpu.VMEM(g.shape, BF16) for g in grads + list(outs[:2])],
            *[pltpu.VMEM(a, F32) for a in shapes],
            pltpu.SemaphoreType.DMA((16,)),
        ],
        compiler_params=pltpu.CompilerParams(vmem_limit_bytes=65400 * 1024),
        name="unpack",
    )(*grads, outs[0], outs[1])
    g_query, g_key, g_value, g_out, g_gate, g_up, g_down, block_out, in_grad = unpacked
    gain_grads = lax.dynamic_slice(gain_grad, (0, lax.rem(ctx_me * R, 128)), (2, R))
    return (
        block_out, in_grad, gain_grads[0], g_query, g_key, g_value, g_out, gain_grads[1], g_gate, g_up, g_down,
    )


def solution(mesh):
    n_ctx, tp = mesh.devices.shape
    Z = 4
    X = 2 if n_ctx == 16 else 4
    YH = n_ctx // (Z * X * 2)
    sizes = (YH, Z, X, tp)
    split = Mesh(mesh.devices.reshape(YH, Z, X, 2, tp), AXES)
    ctx = AXES[:4]
    rows, weight, vector = P(ctx, None), P(ctx, "tp"), P(ctx)
    return jax.shard_map(
        lambda *args: local(sizes, *args),
        mesh=split,
        in_specs=(rows, P(), vector, weight, weight, weight, weight, vector, weight, weight, weight, rows),
        out_specs=(rows, rows, vector, weight, weight, weight, weight, vector, weight, weight, weight),
        check_vma=False,
    )
```
